256 devices in a mesh: row: 16 (over x, y), col: 16 (over z, core).
Axes of the slice: x: 4, y: 4, z: 8, core: 2. Of those that a mesh axis runs over, the one named last changes fastest.
Arguments:
- image_embed: float32 [12288, 768], P(('row', 'col')), may hold values from -40 to 40, as said below
- text_embed: float32 [12288, 768], P(('col', 'row')), may hold values from -40 to 40, as said below
- logit_scale: float32 [1], replicated, may hold values from 120 to 250
Outputs:
- loss: float32 [], replicated
- grad_image: float32 [12288, 768], P(('row', 'col'))
- grad_text: float32 [12288, 768], P(('col', 'row'))
The draws below stay inside these ranges and needn't reach their ends.
Inputs may be any that keep to these rules, and one draw needn't show every extreme that they name: Rows of image_embed have norms spread over a factor of ten; text row i is correlated with image row i, and some pairs point the same way. `text_embed`: some text rows nearly repeat the direction of the row before them.
All inputs are finite; a program needn't handle non-finite values.
Results may differ from the reference program's by a relative error of at most 0.0082.
Values may be sent and summed in bfloat16 or wider, within the bound.
A program may use at most 64 MiB of HBM per device.

```python
import math
import jax
import jax.numpy as jnp
from jax import lax

EMBED = 768
BATCH = 12288


def shared_parts(key):
    center_key, pair_key, group_key, anchor_key, extra_key = jax.random.split(key, 5)
    groups = max(BATCH // 64, 1)
    centers = jax.random.normal(center_key, (groups, EMBED), jnp.float32)
    members = jax.random.randint(group_key, (BATCH,), 0, groups)
    paired = jax.random.normal(pair_key, (BATCH, EMBED), jnp.float32)
    anchor = jax.random.normal(anchor_key, (BATCH, EMBED), jnp.float32)
    extra = jax.random.normal(extra_key, (BATCH, EMBED), jnp.float32)
    return (0.5 * centers[members] + 0.245 * paired, anchor, extra)


def row_scales(key):
    return 0.2 * jnp.exp(jax.random.uniform(key, (BATCH, 1), jnp.float32, 0.0, math.log(10.0)))


def noise_of(key, spread):
    noise = jax.random.normal(key, (BATCH, EMBED), jnp.float32) * spread
    return noise


def draw_image_embed(key, part):
    base, anchor, extra = shared_parts(key)
    key = jax.random.fold_in(key, 11)
    first_key, second_key = jax.random.split(key)
    row_ids = jnp.arange(BATCH)[:, None]
    values = base + noise_of(first_key, 0.83)
    values = jnp.where(row_ids % 97 == 0, anchor, values)
    return jnp.clip(values * row_scales(second_key), -40.0, 40.0)


def draw_text_embed(key, part):
    base, anchor, extra = shared_parts(key)
    key = jax.random.fold_in(key, 23)
    first_key, second_key = jax.random.split(key)
    row_ids = jnp.arange(BATCH)[:, None]
    values = base + noise_of(first_key, 0.83)
    near = jnp.roll(anchor, 1, axis=0) + 0.12 * extra
    values = jnp.where(row_ids % 97 == 1, near, values)
    values = jnp.where(row_ids % 97 == 0, anchor, values)
    return jnp.clip(values * row_scales(second_key), -40.0, 40.0)


def setup_inputs(seed: int = 0) -> dict:
    key_list = jax.random.split(jax.random.key(seed), 4)
    return {
        "image_embed": draw_image_embed(jax.random.fold_in(key_list[3], 71), 0),
        "text_embed": draw_text_embed(jax.random.fold_in(key_list[3], 71), 0),
        "logit_scale": jnp.clip(jnp.exp(jax.random.uniform(key_list[2], (1,), jnp.float32, math.log(120.0), math.log(250.0))), 120.0, 250.0),
    }


eps = 1e-06

def reference(image_embed, text_embed, logit_scale):
    scale = logit_scale[0]
    inv_image = lax.rsqrt(lax.optimization_barrier(jnp.sum(image_embed * image_embed, axis=1, keepdims=True)) + eps)
    inv_text = lax.rsqrt(lax.optimization_barrier(jnp.sum(text_embed * text_embed, axis=1, keepdims=True)) + eps)
    unit_image = image_embed * inv_image
    unit_text = text_embed * inv_text
    low_image = unit_image.astype(jnp.bfloat16)
    low_text = unit_text.astype(jnp.bfloat16)
    block_len = 2048 if BATCH % 2048 == 0 else BATCH
    count = BATCH // block_len
    image_blocks = low_image.reshape(count, block_len, EMBED)
    starts = (jnp.arange(count) * block_len).astype(jnp.int32)
    col_ids = jnp.arange(BATCH).astype(jnp.int32)

    def logits_of(block):
        return scale * lax.dot_general(block, low_text, (((1,), (1,)), ((), ())), preferred_element_type=jnp.float32)

    def forward(carry, inputs):
        col_max, col_sum = carry
        block, first = inputs
        logits = logits_of(block)
        row_max = lax.optimization_barrier(jnp.max(logits, axis=1))
        row_lse = row_max + jnp.log(lax.optimization_barrier(jnp.sum(jnp.exp(logits - row_max[:, None]), axis=1)))
        new_max = jnp.maximum(col_max, lax.optimization_barrier(jnp.max(logits, axis=0)))
        col_sum = col_sum * jnp.exp(col_max - new_max) + lax.optimization_barrier(jnp.sum(jnp.exp(logits - new_max[None, :]), axis=0))
        return ((new_max, col_sum), row_lse)
    init = (jnp.full((BATCH,), -jnp.inf, jnp.float32), jnp.zeros((BATCH,), jnp.float32))
    (col_max, col_sum), row_lse = lax.scan(forward, init, (image_blocks, starts))
    col_lse = col_max + jnp.log(col_sum)
    row_lse = row_lse.reshape(count, block_len)
    diagonal = scale * lax.optimization_barrier(jnp.sum(low_image.astype(jnp.float32) * low_text.astype(jnp.float32), axis=1))
    loss = (jnp.sum(row_lse) + jnp.sum(col_lse) - 2.0 * jnp.sum(diagonal)) / (2.0 * BATCH)

    def backward(grad_text, inputs):
        block, first, lse_rows = inputs
        logits = logits_of(block)
        row_ids = first + jnp.arange(block_len).astype(jnp.int32)
        delta = (row_ids[:, None] == col_ids[None, :]).astype(jnp.float32)
        dlogits = ((jnp.exp(logits - lse_rows[:, None]) + jnp.exp(logits - col_lse[None, :]) - 2.0 * delta) * 0.5).astype(jnp.bfloat16)
        grad_rows = scale * jnp.dot(dlogits, low_text, preferred_element_type=jnp.float32)
        grad_text = grad_text + scale * lax.dot_general(dlogits, block, (((0,), (0,)), ((), ())), preferred_element_type=jnp.float32)
        return (grad_text, grad_rows)
    grad_unit_text, grad_unit_image = lax.scan(backward, jnp.zeros((BATCH, EMBED), jnp.float32), (image_blocks, starts, row_lse))
    grad_unit_image = grad_unit_image.reshape(BATCH, EMBED)
    grad_image = inv_image * (grad_unit_image - unit_image * lax.optimization_barrier(jnp.sum(unit_image * grad_unit_image, axis=1, keepdims=True)))
    grad_text = inv_text * (grad_unit_text - unit_text * lax.optimization_barrier(jnp.sum(unit_text * grad_unit_text, axis=1, keepdims=True)))
    return (loss, grad_image, grad_text)
```

```python
import jax
import jax.numpy as jnp
from jax import lax
from jax.experimental import pallas as pl
from jax.experimental.pallas import tpu as pltpu
from jax.sharding import PartitionSpec as P

EPS = 1e-06
LOG2E = 1.4426950408889634
LN2 = 0.6931471805599453
MESH = pl.DeviceIdType.MESH
F32 = jnp.float32
BF16 = jnp.bfloat16
SHARD, WIDTH, BLOCK, TILE = 48, 768, 768, 128
TILES = BLOCK // TILE
HALF = WIDTH // 2
ROWS, COLS, ZS = 16, 16, 8


def kernel(
    image_hbm, text_hbm, scale_ref, loss_ref, grad_image_ref, grad_text_ref,
    image_in, text_in, image_all, text_all, logits, col_parts, dlogits,
    row_stats, col_stats, row_loss, col_loss,
    image_part, image_other, image_sum, image_hop, image_far, image_half, image_near,
    text_part, text_line, text_hop, text_near,
    in_sem, gather_send, gather_recv, stat_send, stat_recv, reduce_send, reduce_recv,
):
    r = lax.axis_index("row")
    c = lax.axis_index("col")
    x, y = r // 4, r % 4
    z, k = c // 2, c % 2
    a_pos, b_pos = x + k * (y - x), y + k * (x - y)
    a_step, b_step = 4 - 3 * k, 1 + 3 * k

    def line(a, b):
        return a * a_step + b * b_step

    def up(d):
        return (r, ((z + d + ZS) % ZS) * 2 + k)

    def copy(src, dst, send, recv, device):
        return pltpu.make_async_remote_copy(
            src_ref=src, dst_ref=dst, send_sem=send, recv_sem=recv,
            device_id=device, device_id_type=MESH,
        )

    loads = [
        pltpu.make_async_copy(image_hbm, image_in, in_sem.at[0]),
        pltpu.make_async_copy(text_hbm, text_in, in_sem.at[1]),
    ]
    for load in loads:
        load.start()
    barrier = pltpu.get_barrier_semaphore()
    for i in range(1, 16):
        pl.semaphore_signal(barrier, inc=1, device_id=((r + i) % ROWS, c), device_id_type=MESH)
        pl.semaphore_signal(barrier, inc=1, device_id=(r, (c + i) % COLS), device_id_type=MESH)

    def rows_of(ref, index):
        return ref.at[pl.ds(pl.multiple_of(index * SHARD, SHARD), SHARD), :]

    def normalised(ref):
        rows = ref[...]
        inverse = lax.rsqrt(jnp.sum(rows * rows, axis=1, keepdims=True) + EPS)
        return rows * inverse, inverse

    loads[0].wait()
    rows_of(image_all, c)[...] = normalised(image_in)[0].astype(BF16)
    loads[1].wait()
    rows_of(text_all, r)[...] = normalised(text_in)[0].astype(BF16)
    pl.semaphore_wait(barrier, 30)

    started = []

    def gather(src, index, device):
        cp = copy(src, src, gather_send.at[index], gather_recv.at[index], device)
        cp.start()
        started.append(cp)
        return cp

    def image_rows(d):
        return rows_of(image_all, ((z + d + ZS) % ZS) * 2 + k)

    def half_of(block, which):
        return block.at[:, which * HALF:(which + 1) * HALF]

    sibling = (r, z * 2 + 1 - k)
    text_own = rows_of(text_all, r)
    near = {}
    hops = {}
    for d in (2, -2):
        hops[d] = gather(image_rows(0), 2 + d, up(d))
    for a in (2, 1, 3):
        near[a] = gather(text_own, 16 + a, (line((a_pos + a) % 4, b_pos), c))
    for d in (1, -1):
        hops[d] = gather(image_rows(0), 2 + d, up(d))
    shares = [gather(image_rows(0), 7, sibling)]
    across = []

    def pass_text(a):
        block = rows_of(text_all, line((a_pos + 4 - a) % 4, b_pos))
        for b in (2, 1, 3):
            across.append(gather(block, 20 + 4 * a + b, (line(a_pos, (b_pos + b) % 4), c)))

    pass_text(0)
    ends = []
    for d, sign in ((2, 1), (-2, -1)):
        hops[d].wait_recv()
        block = image_rows(-d)
        ends.append(gather(block, 5 + (sign > 0), up(sign)))
        ends.append(gather(half_of(block, 0 if sign > 0 else 1), 36 + (sign > 0), up(d)))
        shares.append(gather(block, 10 + d, sibling))
    for a in (1, 3, 2):
        near[a].wait_recv()
        pass_text(a)
    for d in (1, -1):
        hops[d].wait_recv()
        shares.append(gather(image_rows(-d), 10 + d, sibling))
    ends[0].wait_recv()
    shares.append(gather(image_rows(-3), 13, sibling))
    ends[2].wait_recv()
    shares.append(gather(image_rows(3), 14, sibling))
    ends[1].wait_recv()
    ends[3].wait_recv()
    shares.append(gather(image_rows(4), 15, sibling))
    for cp in across + shares:
        cp.wait_recv()
    for cp in started:
        cp.wait_send()

    scale = scale_ref[0]
    scale2 = scale * LOG2E
    on_diagonal = (r == c).astype(F32)
    eye = lax.broadcasted_iota(jnp.int32, (TILE, TILE), 0) == lax.broadcasted_iota(
        jnp.int32, (TILE, TILE), 1
    )

    def forward(q, diagonal):
        first = pl.multiple_of(q * TILE, TILE)
        block = scale2 * lax.dot_general(
            image_all[pl.ds(first, TILE), :], text_all[...], (((1,), (1,)), ((), ())),
            preferred_element_type=F32,
        )
        logits[pl.ds(first, TILE), :] = block
        row_max = jnp.max(block, axis=1, keepdims=True)
        row_lse = row_max + jnp.log2(jnp.sum(jnp.exp2(block - row_max), axis=1, keepdims=True))
        col_max = jnp.max(block, axis=0, keepdims=True)
        col_lse = col_max + jnp.log2(jnp.sum(jnp.exp2(block - col_max), axis=0, keepdims=True))
        row_stats[0, pl.ds(q, 1), :] = jnp.broadcast_to(row_lse, (TILE, TILE)).T[0:1, :]
        col_parts[pl.ds(q, 1), :] = col_lse
        own = logits[pl.ds(first, TILE), pl.ds(first, TILE)]
        return diagonal + jnp.sum(jnp.where(eye, own, 0.0), axis=0, keepdims=True)

    diagonal = lax.fori_loop(0, TILES, forward, jnp.zeros((1, TILE), F32))
    row_stats[0, 6:8, :] = jnp.concatenate([diagonal * on_diagonal, jnp.zeros((1, TILE), F32)], axis=0)
    parts = col_parts[0:TILES, :]
    top = jnp.max(parts, axis=0, keepdims=True)
    merged = top + jnp.log2(jnp.sum(jnp.exp2(parts - top), axis=0, keepdims=True))
    for q in range(TILES):
        col_stats[0, q:q + 1, :] = merged[:, q * TILE:(q + 1) * TILE]
    col_stats[0, 6:8, :] = jnp.zeros((2, TILE), F32)

    def exchange(to_cols, to_rows, base):
        copies = []
        for i in range(1, 16):
            copies.append(copy(
                to_cols.at[0], to_cols.at[i], stat_send.at[base + i], stat_recv.at[base + i],
                (r, (c + i) % COLS),
            ))
            copies.append(copy(
                to_rows.at[0], to_rows.at[i], stat_send.at[base + 16 + i],
                stat_recv.at[base + 16 + i], ((r + i) % ROWS, c),
            ))
        for cp in copies:
            cp.start()
        return copies

    copies = exchange(row_stats, col_stats, 0)
    for cp in copies:
        cp.wait_recv()

    def merge(stats):
        every = stats[...]
        most = jnp.max(every, axis=0)
        return most + jnp.log2(jnp.sum(jnp.exp2(every - most[None]), axis=0))

    row_lse = merge(row_stats)
    col_lse = merge(col_stats)
    lse_columns = row_lse.T
    diagonal_sum = jnp.sum(row_stats[...], axis=0)[6:7, :]
    for cp in copies:
        cp.wait_send()

    col_row = jnp.concatenate([col_lse[q:q + 1, :] for q in range(TILES)], axis=1)
    for q in range(TILES):
        rows = slice(q * TILE, (q + 1) * TILE)
        block = logits[rows, :]
        total = jnp.exp2(block - lse_columns[:, q:q + 1]) + jnp.exp2(block - col_row)
        dlogits[rows, :] = (0.5 * total).astype(BF16)
        near_own = total[:, rows] - jnp.where(eye, 2.0 * on_diagonal, 0.0)
        dlogits[rows, rows] = (0.5 * near_own).astype(BF16)

    pending = []

    def reduce(src, dst, index, device):
        cp = copy(src, dst, reduce_send.at[index], reduce_recv.at[index], device)
        cp.start()
        pending.append(cp)
        return cp

    def image_terms(q, carry):
        part = scale * jnp.dot(
            dlogits[pl.ds(pl.multiple_of(q * 192, 192), 192), :], text_all[...],
            preferred_element_type=F32,
        )
        image_part[pl.ds(2 * q, 2)] = part.astype(BF16).reshape(2, 2, SHARD, WIDTH)
        return carry

    lax.fori_loop(0, 4, image_terms, 0)
    swap = reduce(image_part.at[:, 1 - k], image_other, 0, sibling)

    for q in range(3):
        rows = slice(q * 256, (q + 1) * 256)
        part = scale * lax.dot_general(
            dlogits[:, rows], image_all[...], (((0,), (0,)), ((), ())), preferred_element_type=F32
        )
        text_part[rows, :] = part.astype(BF16)

    lines = {}
    for b in (2, 1, 3):
        for a in range(4):
            lines[a, b] = reduce(
                rows_of(text_part, line(a, (b_pos + b) % 4)), text_line.at[b - 1, a],
                16 + 4 * b + a, (line(a_pos, (b_pos + b) % 4), c),
            )

    swap.wait_recv()

    def of_z(d):
        index = (z + d + ZS) % ZS
        return image_part[index, k].astype(F32) + image_other[index].astype(F32)

    def send_sum(d):
        image_sum[d % ZS] = of_z(d).astype(BF16)
        return image_sum.at[d % ZS]

    far = {}
    quarter = {}
    direct = {}
    block = send_sum(4)
    for s, sign in ((0, 1), (1, -1)):
        quarter[sign] = reduce(half_of(block, s), image_half.at[s], 1 + s, up(2 * sign))
    for s, sign in ((0, 1), (1, -1)):
        far[sign] = reduce(send_sum(3 * sign), image_far.at[s], 3 + s, up(sign))
    for s, sign in ((0, 1), (1, -1)):
        direct[sign] = reduce(send_sum(sign), image_near.at[s], 5 + s, up(sign))

    total_row = jnp.sum(row_lse[0:6, :], axis=0, keepdims=True) - 2.0 * diagonal_sum
    total_col = jnp.sum(col_lse[0:6, :], axis=0, keepdims=True)
    row_loss[0] = jnp.broadcast_to(total_row, (8, TILE))
    col_loss[0] = jnp.broadcast_to(total_col, (8, TILE))
    loss_copies = exchange(col_loss, row_loss, 32)

    hop = {}
    for s, sign in ((0, 1), (1, -1)):
        far[sign].wait_recv()
        quarter[sign].wait_recv()
        both = of_z(2 * sign) + image_far[s].astype(F32)
        cols = slice(s * HALF, (s + 1) * HALF)
        other = slice((1 - s) * HALF, (2 - s) * HALF)
        slot = image_sum.at[(2 * sign) % ZS]
        slot[:, other] = both[:, other].astype(BF16)
        slot[:, cols] = (both[:, cols] + image_half[s].astype(F32)).astype(BF16)
        hop[sign] = reduce(slot, image_hop.at[s], 7 + s, up(2 * sign))

    for cp in lines.values():
        cp.wait_recv()

    def of_line(a):
        index = (a_pos + a) % 4
        total = rows_of(text_part, line(index, b_pos))[...].astype(F32)
        for b in range(3):
            total = total + text_line[b, index].astype(F32)
        return total

    last = {}
    for a in (2, 1, 3):
        text_hop[a] = of_line(a).astype(BF16)
        last[a] = reduce(
            text_hop.at[a], text_near.at[a], 8 + a, (line((a_pos + a) % 4, b_pos), c)
        )

    def project(ref, gradient):
        unit, inverse = normalised(ref)
        return inverse * (gradient - unit * jnp.sum(unit * gradient, axis=1, keepdims=True))

    gradient = of_z(0)
    for s, sign in ((0, 1), (1, -1)):
        direct[sign].wait_recv()
        gradient = gradient + image_near[s].astype(F32)
    for s, sign in ((0, 1), (1, -1)):
        hop[sign].wait_recv()
        gradient = gradient + image_hop[s].astype(F32)
    grad_image_ref[...] = project(image_in, gradient)

    gradient = of_line(0)
    for a in (2, 1, 3):
        last[a].wait_recv()
        gradient = gradient + text_near[a].astype(F32)
    grad_text_ref[...] = project(text_in, gradient)

    for cp in loss_copies:
        cp.wait_recv()
    sums = jnp.sum(row_loss[...] + col_loss[...], axis=0)[0:1, :]
    loss_ref[...] = jnp.broadcast_to(
        jnp.sum(sums, axis=1, keepdims=True) * (LN2 / (2.0 * ROWS * BLOCK)), (1, TILE)
    )
    for cp in pending + loss_copies:
        cp.wait_send()


def body(image_embed, text_embed, logit_scale):
    loss, grad_image, grad_text = pl.pallas_call(
        kernel,
        name="contrastive",
        out_shape=(
            jax.ShapeDtypeStruct((1, TILE), F32),
            jax.ShapeDtypeStruct((SHARD, WIDTH), F32),
            jax.ShapeDtypeStruct((SHARD, WIDTH), F32),
        ),
        in_specs=[
            pl.BlockSpec(memory_space=pl.ANY),
            pl.BlockSpec(memory_space=pl.ANY),
            pl.BlockSpec(memory_space=pltpu.SMEM),
        ],
        out_specs=(pl.BlockSpec(memory_space=pltpu.VMEM),) * 3,
        scratch_shapes=[
            pltpu.VMEM((SHARD, WIDTH), F32),
            pltpu.VMEM((SHARD, WIDTH), F32),
            pltpu.VMEM((BLOCK, WIDTH), BF16),
            pltpu.VMEM((BLOCK, WIDTH), BF16),
            pltpu.VMEM((BLOCK, BLOCK), F32),
            pltpu.VMEM((8, BLOCK), F32),
            pltpu.VMEM((BLOCK, BLOCK), BF16),
            pltpu.VMEM((16, 8, TILE), F32),
            pltpu.VMEM((16, 8, TILE), F32),
            pltpu.VMEM((16, 8, TILE), F32),
            pltpu.VMEM((16, 8, TILE), F32),
            pltpu.VMEM((ZS, 2, SHARD, WIDTH), BF16),
            pltpu.VMEM((ZS, SHARD, WIDTH), BF16),
            pltpu.VMEM((ZS, SHARD, WIDTH), BF16),
            pltpu.VMEM((2, SHARD, WIDTH), BF16),
            pltpu.VMEM((2, SHARD, WIDTH), BF16),
            pltpu.VMEM((2, SHARD, HALF), BF16),
            pltpu.VMEM((2, SHARD, WIDTH), BF16),
            pltpu.VMEM((BLOCK, WIDTH), BF16),
            pltpu.VMEM((3, 4, SHARD, WIDTH), BF16),
            pltpu.VMEM((4, SHARD, WIDTH), BF16),
            pltpu.VMEM((4, SHARD, WIDTH), BF16),
            pltpu.SemaphoreType.DMA((2,)),
            pltpu.SemaphoreType.DMA((40,)),
            pltpu.SemaphoreType.DMA((40,)),
            pltpu.SemaphoreType.DMA((64,)),
            pltpu.SemaphoreType.DMA((64,)),
            pltpu.SemaphoreType.DMA((32,)),
            pltpu.SemaphoreType.DMA((32,)),
        ],
        compiler_params=pltpu.CompilerParams(
            collective_id=0, has_side_effects=True, vmem_limit_bytes=48 << 20
        ),
    )(image_embed, text_embed, logit_scale)
    return loss[0, 0], grad_image, grad_text


def solution(mesh):
    placed = (P(("row", "col"), None), P(("col", "row"), None), P())
    return jax.shard_map(
        body,
        mesh=mesh,
        in_specs=placed,
        out_specs=(P(), P(("row", "col"), None), P(("col", "row"), None)),
        check_vma=False,
    )
```

```python
import jax
import jax.numpy as jnp
from jax import lax
from jax.experimental import pallas as pl
from jax.experimental.pallas import tpu as pltpu
from jax.sharding import PartitionSpec as P

EPS = 1e-06
LOG2E = 1.4426950408889634
LN2 = 0.6931471805599453
MESH = pl.DeviceIdType.MESH
F32 = jnp.float32
BF16 = jnp.bfloat16
SHARD, WIDTH, BLOCK, LANES = 48, 768, 768, 128
PAIR = 2 * SHARD
HALF = WIDTH // 2
ROWS, COLS, ZS = 16, 16, 8
ORDER = (4, 3, -3, 2, -2, 1, -1, 0)
SLOT = {d: s for s, d in enumerate(ORDER)} | {-4: 0}


def kernel(
    image_hbm, text_hbm, scale_ref, loss_ref, grad_image_ref, grad_text_ref,
    image_unit, text_unit, image_inv, text_inv, image_all, text_all, logits, col_parts, dlogits,
    row_stats, col_stats, row_merged, loss_a, loss_b,
    image_part, image_other, image_sum, image_hop, image_far, image_half, image_near,
    text_part, text_line, text_hop, text_near,
    in_sem, gather_send, gather_recv, stat_sem, reduce_send, reduce_recv,
):
    r = lax.axis_index("row")
    c = lax.axis_index("col")
    x, y = r // 4, r % 4
    z, k = c // 2, c % 2
    a_pos, b_pos = x + k * (y - x), y + k * (x - y)
    a_step, b_step = 4 - 3 * k, 1 + 3 * k

    def line(a, b):
        return a * a_step + b * b_step

    def on_a(a):
        return (line((a_pos + a) % 4, b_pos), c)

    def on_b(b):
        return (line(a_pos, (b_pos + b) % 4), c)

    def up(d):
        return (r, ((z + d + ZS) % ZS) * 2 + k)

    sibling = (r, z * 2 + 1 - k)

    def copy(src, dst, send, recv, device):
        return pltpu.make_async_remote_copy(
            src_ref=src, dst_ref=dst, send_sem=send, recv_sem=recv,
            device_id=device, device_id_type=MESH,
        )

    loads = [
        pltpu.make_async_copy(image_hbm, image_unit, in_sem.at[0]),
        pltpu.make_async_copy(text_hbm, text_unit, in_sem.at[1]),
    ]
    for load in loads:
        load.start()
    barrier = pltpu.get_barrier_semaphore()
    partners = [up(d) for d in (2, -2, 1, -1)] + [sibling]
    partners += [on_a(a) for a in (1, 2, 3)] + [on_b(b) for b in (1, 2, 3)]
    for device in partners:
        pl.semaphore_signal(barrier, inc=1, device_id=device, device_id_type=MESH)

    def text_rows(index):
        return text_all.at[pl.ds(pl.multiple_of(index * SHARD, SHARD), SHARD), :]

    def image_rows(d):
        first = SLOT[d] * PAIR + k * SHARD
        return image_all.at[pl.ds(pl.multiple_of(first, SHARD), SHARD), :]

    def normalise(ref, inv_ref):
        rows = ref[...]
        inverse = lax.rsqrt(jnp.sum(rows * rows, axis=1, keepdims=True) + EPS)
        unit = rows * inverse
        ref[...] = unit
        inv_ref[...] = jnp.broadcast_to(inverse, (SHARD, LANES))
        return unit.astype(BF16)

    loads[0].wait()
    image_rows(0)[...] = normalise(image_unit, image_inv)
    loads[1].wait()
    text_rows(r)[...] = normalise(text_unit, text_inv)
    row_stats[0] = jnp.zeros((8, LANES), F32)
    col_stats[0] = jnp.zeros((8, LANES), F32)
    pl.semaphore_wait(barrier, len(partners))

    started = []

    def gather(src, dst, index, device):
        cp = copy(src, dst, gather_send.at[index], gather_recv.at[index], device)
        cp.start()
        started.append(cp)
        return cp

    def half_of(block, which):
        return block.at[:, which * HALF:(which + 1) * HALF]

    def share(d, index):
        return gather(image_rows(d), image_rows(d), index, sibling)

    text_own = text_rows(r)
    near = {}
    hops = {}
    across = []
    for d in (2, -2):
        hops[d] = gather(image_rows(0), image_rows(-d), 2 + d, up(d))
    for a in (2, 1, 3):
        near[a] = gather(text_own, text_own, 16 + a, on_a(a))
    for d in (1, -1):
        hops[d] = gather(image_rows(0), image_rows(-d), 2 + d, up(d))
    shares = [share(0, 7)]

    def pass_text(a):
        block = text_rows(line((a_pos + 4 - a) % 4, b_pos))
        for b in (2, 1, 3):
            across.append(gather(block, block, 20 + 4 * a + b, on_b(b)))

    pass_text(0)
    ends = []
    for d, sign in ((2, 1), (-2, -1)):
        hops[d].wait_recv()
        block = image_rows(-d)
        ends.append(gather(block, image_rows(-d - sign), 5 + (sign > 0), up(sign)))
        s = 0 if sign > 0 else 1
        ends.append(gather(half_of(block, s), half_of(image_rows(4), s), 36 + s, up(d)))
        shares.append(share(-d, 10 + d))
    for a in (1, 3, 2):
        near[a].wait_recv()
        pass_text(a)
    for d in (1, -1):
        hops[d].wait_recv()
        shares.append(share(-d, 10 + d))
    ends[0].wait_recv()
    shares.append(share(-3, 13))
    ends[2].wait_recv()
    shares.append(share(3, 14))
    ends[1].wait_recv()
    ends[3].wait_recv()
    shares.append(share(4, 15))
    for cp in across + shares:
        cp.wait_recv()

    scale2 = scale_ref[0] * LOG2E
    apart = lax.broadcasted_iota(jnp.int32, (PAIR, BLOCK), 1) - lax.broadcasted_iota(
        jnp.int32, (PAIR, BLOCK), 0
    )
    lane = lax.broadcasted_iota(jnp.int32, (PAIR, LANES), 1)
    off_diagonal = (r != c).astype(jnp.int32) * (2 * BLOCK)

    def z_of(d):
        return (z + d + ZS) % ZS

    def own_pairs(s):
        return apart == z_of(ORDER[s]) * PAIR + off_diagonal

    row_lse = jnp.zeros((PAIR, LANES), F32)
    diagonal = jnp.zeros((1, BLOCK), F32)
    for h in range(2):
        rows = slice(h * HALF, (h + 1) * HALF)
        logits[rows, :] = scale2 * lax.dot_general(
            image_all[rows, :], text_all[...], (((1,), (1,)), ((), ())),
            preferred_element_type=F32,
        )
        for s in range(4 * h, 4 * h + 4):
            block = logits[s * PAIR:(s + 1) * PAIR, :]
            row_max = jnp.max(block, axis=1, keepdims=True)
            row_sum = jnp.sum(jnp.exp2(block - row_max), axis=1, keepdims=True)
            row_lse = jnp.where(lane == s, row_max + jnp.log2(row_sum), row_lse)
            col_max = jnp.max(block, axis=0, keepdims=True)
            col_sum = jnp.sum(jnp.exp2(block - col_max), axis=0, keepdims=True)
            col_parts[s:s + 1, :] = col_max + jnp.log2(col_sum)
    row_lse = row_lse.T
    for s in range(ZS):
        row_stats[0, pl.ds(z_of(ORDER[s]), 1), 0:PAIR] = row_lse[s:s + 1, :]
    parts = col_parts[...]
    top = jnp.max(parts, axis=0, keepdims=True)
    merged = top + jnp.log2(jnp.sum(jnp.exp2(parts - top), axis=0, keepdims=True))
    for q in range(6):
        col_stats[0, q:q + 1, :] = merged[:, q * LANES:(q + 1) * LANES]

    def col_peer(i):
        return (r, (c + i) % COLS)

    def row_peer(i):
        return ((r + i) % ROWS, c)

    def spread(ref, sem, peer):
        for i in range(1, 16):
            copy(ref.at[0], ref.at[i], stat_sem.at[2 * sem], stat_sem.at[2 * sem + 1], peer(i)).start()

    def others(ref, sem):
        return pltpu.make_async_copy(ref.at[1:16], ref.at[1:16], stat_sem.at[sem])

    spread(row_stats, 0, col_peer)
    spread(col_stats, 1, row_peer)
    for s in range(ZS):
        block = logits[s * PAIR:(s + 1) * PAIR, :]
        diagonal = diagonal + jnp.sum(jnp.where(own_pairs(s), block, 0.0), axis=0, keepdims=True)
    others(row_stats, 1).wait()
    others(col_stats, 3).wait()

    def merge(stats):
        every = stats[...]
        most = jnp.max(every, axis=0)
        return most + jnp.log2(jnp.sum(jnp.exp2(every - most[None]), axis=0))

    row_merged[...] = merge(row_stats)
    col_lse = merge(col_stats)
    ordered = jnp.concatenate([row_merged[pl.ds(z_of(d), 1), :] for d in ORDER], axis=0)
    lse_columns = ordered.T
    col_row = jnp.concatenate([col_lse[q:q + 1, :] for q in range(6)], axis=1)

    pending = []

    def reduce(src, dst, index, device):
        cp = copy(src, dst, reduce_send.at[index], reduce_recv.at[index], device)
        cp.start()
        pending.append(cp)
        return cp

    swaps = []
    for t in range(4):
        for s in (2 * t, 2 * t + 1):
            rows = slice(s * PAIR, (s + 1) * PAIR)
            block = logits[rows, :]
            total = jnp.exp2(block - lse_columns[0:PAIR, s:s + 1]) + jnp.exp2(block - col_row)
            total = total - jnp.where(own_pairs(s), 2.0, 0.0)
            dlogits[rows, :] = (0.5 * total).astype(BF16)
        part = jnp.dot(
            dlogits[2 * t * PAIR:(2 * t + 2) * PAIR, :], text_all[...], preferred_element_type=F32
        )
        image_part[2 * t:2 * t + 2] = part.astype(BF16).reshape(2, 2, SHARD, WIDTH)
        swaps.append(reduce(
            image_part.at[2 * t:2 * t + 2, 1 - k], image_other.at[2 * t:2 * t + 2], 12 + t, sibling
        ))

    def text_terms(h):
        rows = slice(h * HALF, (h + 1) * HALF)
        part = lax.dot_general(
            dlogits[:, rows], image_all[...], (((0,), (0,)), ((), ())), preferred_element_type=F32
        )
        text_part[rows, :] = part.astype(BF16)

    def of_z(d):
        s = SLOT[d]
        return image_part[s, k].astype(F32) + image_other[s].astype(F32)

    def summed(d):
        image_sum[SLOT[d]] = of_z(d).astype(BF16)
        return image_sum.at[SLOT[d]]

    quarter = {}
    far = {}
    direct = {}
    text_terms(0)
    swaps[0].wait_recv()
    block = summed(4)
    for s, sign in ((0, 1), (1, -1)):
        quarter[sign] = reduce(half_of(block, s), image_half.at[s], 1 + s, up(2 * sign))
    far[1] = reduce(summed(3), image_far.at[0], 3, up(1))
    text_terms(1)
    lines = {}
    for b in (2, 1, 3):
        for a in range(4):
            lines[a, b] = reduce(
                text_rows_of(text_part, line(a, (b_pos + b) % 4)), text_line.at[b - 1, a],
                16 + 4 * b + a, on_b(b),
            )
    swaps[1].wait_recv()
    far[-1] = reduce(summed(-3), image_far.at[1], 4, up(-1))
    swaps[2].wait_recv()
    direct[1] = reduce(summed(1), image_near.at[0], 5, up(1))
    swaps[3].wait_recv()
    direct[-1] = reduce(summed(-1), image_near.at[1], 6, up(-1))

    col_total = jnp.sum(col_lse[0:6, :], axis=0, keepdims=True)
    on_block = jnp.sum(diagonal, axis=1, keepdims=True)
    loss_a[0] = jnp.concatenate(
        [col_total, jnp.broadcast_to(on_block, (1, LANES)), jnp.zeros((6, LANES), F32)], axis=0
    )
    spread(loss_a, 2, col_peer)

    hop = {}
    for s, sign in ((0, 1), (1, -1)):
        far[sign].wait_recv()
        quarter[sign].wait_recv()
        both = of_z(2 * sign) + image_far[s].astype(F32)
        cols = slice(s * HALF, (s + 1) * HALF)
        rest = slice((1 - s) * HALF, (2 - s) * HALF)
        slot = image_sum.at[SLOT[2 * sign]]
        slot[:, rest] = both[:, rest].astype(BF16)
        slot[:, cols] = (both[:, cols] + image_half[s].astype(F32)).astype(BF16)
        hop[sign] = reduce(slot, image_hop.at[s], 7 + s, up(2 * sign))

    for cp in lines.values():
        cp.wait_recv()

    def of_line(a):
        index = (a_pos + a) % 4
        total = text_rows_of(text_part, line(index, b_pos))[...].astype(F32)
        for b in range(3):
            total = total + text_line[b, index].astype(F32)
        return total

    last = {}
    for a in (2, 1, 3):
        text_hop[a] = of_line(a).astype(BF16)
        last[a] = reduce(text_hop.at[a], text_near.at[a], 8 + a, on_a(a))

    others(loss_a, 5).wait()
    sums = jnp.sum(loss_a[...], axis=0)
    row_total = jnp.sum(row_merged[:, 0:PAIR], axis=0, keepdims=True)
    row_total = jnp.sum(row_total, axis=1, keepdims=True) - 2.0 * sums[1:2, 0:1]
    loss_b[0] = jnp.broadcast_to(row_total, (8, LANES))
    spread(loss_b, 3, row_peer)

    def project(unit_ref, inv_ref, gradient):
        unit = unit_ref[...]
        along = jnp.sum(unit * gradient, axis=1, keepdims=True)
        return inv_ref[:, 0:1] * (gradient - unit * along)

    gradient = of_z(0)
    for s, sign in ((0, 1), (1, -1)):
        direct[sign].wait_recv()
        gradient = gradient + image_near[s].astype(F32)
    for s, sign in ((0, 1), (1, -1)):
        hop[sign].wait_recv()
        gradient = gradient + image_hop[s].astype(F32)
    grad_image_ref[...] = project(image_unit, image_inv, gradient)

    gradient = of_line(0)
    for a in (2, 1, 3):
        last[a].wait_recv()
        gradient = gradient + text_near[a].astype(F32)
    grad_text_ref[...] = project(text_unit, text_inv, gradient)

    others(loss_b, 7).wait()
    total = jnp.sum(sums[0:1, :], axis=1, keepdims=True) + jnp.sum(loss_b[...], axis=0)[0:1, 0:1]
    loss_ref[...] = jnp.broadcast_to(total * (LN2 / (2.0 * ROWS * BLOCK)), (1, LANES))
    for cp in started + pending:
        cp.wait_send()
    for sem, ref in enumerate((row_stats, col_stats, loss_a, loss_b)):
        others(ref, 2 * sem).wait()


def text_rows_of(ref, index):
    return ref.at[pl.ds(pl.multiple_of(index * SHARD, SHARD), SHARD), :]


def body(image_embed, text_embed, logit_scale):
    loss, grad_image, grad_text = pl.pallas_call(
        kernel,
        name="contrastive",
        out_shape=(
            jax.ShapeDtypeStruct((1, LANES), F32),
            jax.ShapeDtypeStruct((SHARD, WIDTH), F32),
            jax.ShapeDtypeStruct((SHARD, WIDTH), F32),
        ),
        in_specs=[
            pl.BlockSpec(memory_space=pl.ANY),
            pl.BlockSpec(memory_space=pl.ANY),
            pl.BlockSpec(memory_space=pltpu.SMEM),
        ],
        out_specs=(pl.BlockSpec(memory_space=pltpu.VMEM),) * 3,
        scratch_shapes=[
            pltpu.VMEM((SHARD, WIDTH), F32),
            pltpu.VMEM((SHARD, WIDTH), F32),
            pltpu.VMEM((SHARD, LANES), F32),
            pltpu.VMEM((SHARD, LANES), F32),
            pltpu.VMEM((BLOCK, WIDTH), BF16),
            pltpu.VMEM((BLOCK, WIDTH), BF16),
            pltpu.VMEM((BLOCK, BLOCK), F32),
            pltpu.VMEM((ZS, BLOCK), F32),
            pltpu.VMEM((BLOCK, BLOCK), BF16),
            pltpu.VMEM((16, 8, LANES), F32),
            pltpu.VMEM((16, 8, LANES), F32),
            pltpu.VMEM((8, LANES), F32),
            pltpu.VMEM((16, 8, LANES), F32),
            pltpu.VMEM((16, 8, LANES), F32),
            pltpu.VMEM((ZS, 2, SHARD, WIDTH), BF16),
            pltpu.VMEM((ZS, SHARD, WIDTH), BF16),
            pltpu.VMEM((ZS, SHARD, WIDTH), BF16),
            pltpu.VMEM((2, SHARD, WIDTH), BF16),
            pltpu.VMEM((2, SHARD, WIDTH), BF16),
            pltpu.VMEM((2, SHARD, HALF), BF16),
            pltpu.VMEM((2, SHARD, WIDTH), BF16),
            pltpu.VMEM((BLOCK, WIDTH), BF16),
            pltpu.VMEM((3, 4, SHARD, WIDTH), BF16),
            pltpu.VMEM((4, SHARD, WIDTH), BF16),
            pltpu.VMEM((4, SHARD, WIDTH), BF16),
            pltpu.SemaphoreType.DMA((2,)),
            pltpu.SemaphoreType.DMA((40,)),
            pltpu.SemaphoreType.DMA((40,)),
            pltpu.SemaphoreType.DMA((8,)),
            pltpu.SemaphoreType.DMA((32,)),
            pltpu.SemaphoreType.DMA((32,)),
        ],
        compiler_params=pltpu.CompilerParams(
            collective_id=0, has_side_effects=True, vmem_limit_bytes=60 << 20
        ),
    )(image_embed, text_embed, logit_scale)
    scale = logit_scale[0]
    return loss[0, 0], scale * grad_image, scale * grad_text


def solution(mesh):
    placed = (P(("row", "col"), None), P(("col", "row"), None), P())
    return jax.shard_map(
        body,
        mesh=mesh,
        in_specs=placed,
        out_specs=(P(), P(("row", "col"), None), P(("col", "row"), None)),
        check_vma=False,
    )
```

```python
import jax
import jax.numpy as jnp
from jax import lax
from jax.experimental import pallas as pl
from jax.experimental.pallas import tpu as pltpu
from jax.sharding import PartitionSpec as P

EPS = 1e-06
LOG2E = 1.4426950408889634
LN2 = 0.6931471805599453
MESH = pl.DeviceIdType.MESH
F32 = jnp.float32
BF16 = jnp.bfloat16
SHARD, WIDTH, BLOCK, LANES = 48, 768, 768, 128
PAIR = 2 * SHARD
HALF = WIDTH // 2
ROWS, COLS, ZS = 16, 16, 8
ORDER = (4, 3, -3, 2, -2, 1, -1, 0)
SLOT = {d: s for s, d in enumerate(ORDER)} | {-4: 0}


def kernel(
    image_hbm, text_hbm, scale_ref, loss_ref, grad_image_ref, grad_text_ref,
    image_unit, text_unit, image_inv, text_inv, image_all, text_all, logits, col_parts, dlogits,
    row_stats, col_stats, row_merged, loss_a, loss_b,
    image_part, image_other, image_sum, image_hop, image_far, image_half, image_near,
    text_part, text_line, text_hop, text_near,
    in_sem, gather_send, gather_recv, stat_sem, reduce_send, reduce_recv,
):
    r = lax.axis_index("row")
    c = lax.axis_index("col")
    x, y = r // 4, r % 4
    z, k = c // 2, c % 2
    a_pos, b_pos = x + k * (y - x), y + k * (x - y)
    a_step, b_step = 4 - 3 * k, 1 + 3 * k

    def line(a, b):
        return a * a_step + b * b_step

    def on_a(a):
        return (line((a_pos + a) % 4, b_pos), c)

    def on_b(b):
        return (line(a_pos, (b_pos + b) % 4), c)

    def up(d):
        return (r, ((z + d + ZS) % ZS) * 2 + k)

    sibling = (r, z * 2 + 1 - k)

    def copy(src, dst, send, recv, device):
        return pltpu.make_async_remote_copy(
            src_ref=src, dst_ref=dst, send_sem=send, recv_sem=recv,
            device_id=device, device_id_type=MESH,
        )

    loads = [
        pltpu.make_async_copy(image_hbm, image_unit, in_sem.at[0]),
        pltpu.make_async_copy(text_hbm, text_unit, in_sem.at[1]),
    ]
    for load in loads:
        load.start()
    barrier = pltpu.get_barrier_semaphore()
    partners = [up(d) for d in (2, -2, 1, -1)] + [sibling]
    partners += [on_a(a) for a in (1, 2, 3)] + [on_b(b) for b in (1, 2, 3)]
    for device in partners:
        pl.semaphore_signal(barrier, inc=1, device_id=device, device_id_type=MESH)

    def text_rows(index):
        return text_all.at[pl.ds(pl.multiple_of(index * SHARD, SHARD), SHARD), :]

    def image_rows(d):
        first = SLOT[d] * PAIR + k * SHARD
        return image_all.at[pl.ds(pl.multiple_of(first, SHARD), SHARD), :]

    def normalise(ref, inv_ref):
        rows = ref[...]
        inverse = lax.rsqrt(jnp.sum(rows * rows, axis=1, keepdims=True) + EPS)
        unit = rows * inverse
        ref[...] = unit
        inv_ref[...] = jnp.broadcast_to(inverse, (SHARD, LANES))
        return unit.astype(BF16)

    row_stats[0] = jnp.zeros((8, LANES), F32)
    col_stats[0] = jnp.zeros((8, LANES), F32)
    loads[0].wait()
    image_rows(0)[...] = normalise(image_unit, image_inv)
    pl.semaphore_wait(barrier, len(partners))

    started = []

    def gather(src, dst, index, device):
        cp = copy(src, dst, gather_send.at[index], gather_recv.at[index], device)
        cp.start()
        started.append(cp)
        return cp

    def half_of(block, which):
        return block.at[:, which * HALF:(which + 1) * HALF]

    def share(d, index):
        return gather(image_rows(d), image_rows(d), index, sibling)

    sides = ((0, 1), (1, -1))
    ahead = {}
    hops = {}
    near = {}
    across = []
    ends = []
    for turn in range(2):
        for s, sign in sides:
            h = (s + turn) % 2
            ahead[turn, sign] = gather(
                half_of(image_rows(0), h), half_of(image_rows(-2 * sign), h), 4 * s + turn, up(2 * sign)
            )
    loads[1].wait()
    text_own = text_rows(r)
    text_own[...] = normalise(text_unit, text_inv)
    for a in (1, 3, 2):
        near[a] = gather(text_own, text_own, 16 + a, on_a(a))
    for s, sign in sides:
        hops[sign] = gather(image_rows(0), image_rows(-sign), 4 * s + 2, up(sign))

    def pass_text(a):
        block = text_rows(line((a_pos + 4 - a) % 4, b_pos))
        for b in (2, 1, 3):
            across.append(gather(block, block, 20 + 4 * a + b, on_b(b)))

    pass_text(0)
    shares = [share(0, 8)]

    def pass_image(turn):
        for s, sign in sides:
            h = (s + turn) % 2
            ahead[turn, sign].wait_recv()
            block = half_of(image_rows(-2 * sign), h)
            if turn == 0:
                ends.append(gather(block, half_of(image_rows(4), h), 36 + s, up(2 * sign)))
            ends.append(gather(block, half_of(image_rows(-3 * sign), h), 38 + 2 * s + turn, up(sign)))

    for a in (1, 3):
        near[a].wait_recv()
        pass_text(a)
    pass_image(0)
    near[2].wait_recv()
    pass_text(2)
    for s, sign in sides:
        hops[sign].wait_recv()
        shares.append(share(-sign, 9 + s))
    pass_image(1)
    for s, sign in sides:
        shares.append(share(-2 * sign, 11 + s))
    for cp in ends:
        cp.wait_recv()
    for d, index in ((3, 13), (-3, 14), (4, 15)):
        shares.append(share(d, index))
    for cp in across + shares:
        cp.wait_recv()

    scale = scale_ref[0]
    scale2 = scale * LOG2E
    apart = lax.broadcasted_iota(jnp.int32, (PAIR, BLOCK), 1) - lax.broadcasted_iota(
        jnp.int32, (PAIR, BLOCK), 0
    )
    lane = lax.broadcasted_iota(jnp.int32, (PAIR, LANES), 1)
    off_diagonal = (r != c).astype(jnp.int32) * (2 * BLOCK)

    def z_of(d):
        return (z + d + ZS) % ZS

    def own_pairs(s):
        return apart == z_of(ORDER[s]) * PAIR + off_diagonal

    row_lse = jnp.zeros((PAIR, LANES), F32)
    diagonal = jnp.zeros((1, BLOCK), F32)
    for h in range(2):
        rows = slice(h * HALF, (h + 1) * HALF)
        logits[rows, :] = scale2 * lax.dot_general(
            image_all[rows, :], text_all[...], (((1,), (1,)), ((), ())),
            preferred_element_type=F32,
        )
        for s in range(4 * h, 4 * h + 4):
            block = logits[s * PAIR:(s + 1) * PAIR, :]
            row_max = jnp.max(block, axis=1, keepdims=True)
            row_sum = jnp.sum(jnp.exp2(block - row_max), axis=1, keepdims=True)
            row_lse = jnp.where(lane == s, row_max + jnp.log2(row_sum), row_lse)
            col_max = jnp.max(block, axis=0, keepdims=True)
            col_sum = jnp.sum(jnp.exp2(block - col_max), axis=0, keepdims=True)
            col_parts[s:s + 1, :] = col_max + jnp.log2(col_sum)
    row_lse = row_lse.T
    for s in range(ZS):
        row_stats[0, pl.ds(z_of(ORDER[s]), 1), 0:PAIR] = row_lse[s:s + 1, :]
    parts = col_parts[...]
    top = jnp.max(parts, axis=0, keepdims=True)
    merged = top + jnp.log2(jnp.sum(jnp.exp2(parts - top), axis=0, keepdims=True))
    for q in range(6):
        col_stats[0, q:q + 1, :] = merged[:, q * LANES:(q + 1) * LANES]

    col_offsets = [(d, other) for d in ORDER for other in (0, 1) if (d, other) != (0, 0)]
    row_offsets = [(a, b) for a in (2, 1, 3, 0) for b in (2, 1, 3, 0) if (a, b) != (0, 0)]
    row_offsets.sort(key=lambda ab: -min(ab[0], 4 - ab[0]) - min(ab[1], 4 - ab[1]))

    def col_peer(i):
        d, other = col_offsets[i]
        return (r, z_of(d) * 2 + (k + other) % 2)

    def row_peer(i):
        a, b = row_offsets[i]
        return (line((a_pos + a) % 4, (b_pos + b) % 4), c)

    def send_to(ref, sem, peer, i):
        copy(
            ref.at[0], ref.at[i + 1], stat_sem.at[2 * sem], stat_sem.at[2 * sem + 1], peer(i)
        ).start()

    def spread(ref, sem, peer):
        for i in range(15):
            send_to(ref, sem, peer, i)

    def others(ref, sem):
        return pltpu.make_async_copy(ref.at[1:16], ref.at[1:16], stat_sem.at[sem])

    def combine(every):
        most = jnp.max(every, axis=0)
        return most + jnp.log2(jnp.sum(jnp.exp2(every - most[None]), axis=0))

    for i in range(15):
        send_to(row_stats, 0, col_peer, i)
        send_to(col_stats, 1, row_peer, i)
    for s in range(ZS):
        block = logits[s * PAIR:(s + 1) * PAIR, :]
        diagonal = diagonal + jnp.sum(jnp.where(own_pairs(s), block, 0.0), axis=0, keepdims=True)
    others(row_stats, 1).wait()
    others(col_stats, 3).wait()

    row_merged[...] = combine(row_stats[...])
    col_lse = combine(col_stats[...])
    ordered = jnp.concatenate([row_merged[pl.ds(z_of(d), 1), :] for d in ORDER], axis=0)
    lse_columns = ordered.T
    col_row = jnp.concatenate([col_lse[q:q + 1, :] for q in range(6)], axis=1)

    pending = []

    def reduce(src, dst, index, device):
        cp = copy(src, dst, reduce_send.at[index], reduce_recv.at[index], device)
        cp.start()
        pending.append(cp)
        return cp

    def gradient_of(t):
        for s in (2 * t, 2 * t + 1):
            rows = slice(s * PAIR, (s + 1) * PAIR)
            block = logits[rows, :]
            total = jnp.exp2(block - lse_columns[0:PAIR, s:s + 1]) + jnp.exp2(block - col_row)
            total = total - jnp.where(own_pairs(s), 2.0, 0.0)
            dlogits[rows, :] = (0.5 * total).astype(BF16)

    swaps = {}

    def image_terms(t):
        part = scale * jnp.dot(
            dlogits[2 * t * PAIR:(2 * t + 2) * PAIR, :], text_all[...], preferred_element_type=F32
        )
        image_part[2 * t:2 * t + 2] = part.astype(BF16).reshape(2, 2, SHARD, WIDTH)
        swaps[t] = reduce(
            image_part.at[2 * t:2 * t + 2, 1 - k], image_other.at[2 * t:2 * t + 2], 12 + t, sibling
        )

    def text_terms(h):
        rows = slice(h * HALF, (h + 1) * HALF)
        part = scale * lax.dot_general(
            dlogits[:, rows], image_all[...], (((0,), (0,)), ((), ())), preferred_element_type=F32
        )
        text_part[rows, :] = part.astype(BF16)

    def of_z(d):
        s = SLOT[d]
        return image_part[s, k].astype(F32) + image_other[s].astype(F32)

    def summed(d):
        image_sum[SLOT[d]] = of_z(d).astype(BF16)
        return image_sum.at[SLOT[d]]

    quarter = {}
    far = {}
    direct = {}
    gradient_of(0)
    image_terms(0)
    gradient_of(1)
    image_terms(1)
    gradient_of(2)
    gradient_of(3)
    text_terms(0)
    swaps[0].wait_recv()
    swaps[1].wait_recv()
    for s, sign in sides:
        far[sign] = reduce(summed(3 * sign), image_far.at[s], 3 + s, up(sign))
    block = summed(4)
    for s, sign in sides:
        quarter[sign] = reduce(half_of(block, s), image_half.at[s], 1 + s, up(2 * sign))
    text_terms(1)
    lines = {}
    for a in (2, 1, 3, 0):
        for b in (2, 1, 3):
            lines[a, b] = reduce(
                text_rows_of(text_part, line((a_pos + a) % 4, (b_pos + b) % 4)),
                text_line.at[b - 1, a], 16 + 4 * b + a, on_b(b),
            )
    col_total = jnp.sum(col_lse[0:6, :], axis=0, keepdims=True)
    on_block = jnp.sum(diagonal, axis=1, keepdims=True)
    loss_a[0] = jnp.concatenate(
        [col_total, jnp.broadcast_to(on_block, (1, LANES)), jnp.zeros((6, LANES), F32)], axis=0
    )
    spread(loss_a, 2, col_peer)

    image_terms(2)
    image_terms(3)
    swaps[2].wait_recv()
    direct[1] = reduce(summed(1), image_near.at[0], 5, up(1))
    swaps[3].wait_recv()
    direct[-1] = reduce(summed(-1), image_near.at[1], 6, up(-1))

    def of_line(a):
        for b in (1, 2, 3):
            lines[a, b].wait_recv()
        total = text_rows_of(text_part, line((a_pos + a) % 4, b_pos))[...].astype(F32)
        for b in range(3):
            total = total + text_line[b, a].astype(F32)
        return total

    last = {}

    def pass_line(a):
        text_hop[a] = of_line(a).astype(BF16)
        last[a] = reduce(text_hop.at[a], text_near.at[a], 8 + a, on_a(a))

    hop = {}

    def pass_sum(sign, s, half, early):
        cols = slice(half * HALF, (half + 1) * HALF)
        at = SLOT[2 * sign]
        both = image_part[at, k, :, cols].astype(F32) + image_other[at, :, cols].astype(F32)
        both = both + image_far[s, :, cols].astype(F32)
        if not early:
            both = both + image_half[s].astype(F32)
        image_sum[at, :, cols] = both.astype(BF16)
        hop[sign, early] = reduce(
            image_sum.at[at, :, cols], image_hop.at[s, :, cols], 7 + s if early else 17 + s, up(2 * sign)
        )

    for s, sign in sides:
        far[sign].wait_recv()
        pass_sum(sign, s, 1 - s, True)
    pass_line(2)
    others(loss_a, 5).wait()
    sums = jnp.sum(loss_a[...], axis=0)
    row_total = jnp.sum(row_merged[:, 0:PAIR], axis=0, keepdims=True)
    row_total = jnp.sum(row_total, axis=1, keepdims=True) - 2.0 * sums[1:2, 0:1]
    loss_b[0] = jnp.broadcast_to(row_total, (8, LANES))
    spread(loss_b, 3, row_peer)

    for s, sign in sides:
        quarter[sign].wait_recv()
        pass_sum(sign, s, s, False)
    pass_line(1)

    pass_line(3)

    def project(unit_ref, inv_ref, gradient):
        unit = unit_ref[...]
        along = jnp.sum(unit * gradient, axis=1, keepdims=True)
        return inv_ref[:, 0:1] * (gradient - unit * along)

    gradient = of_z(0)
    for s, sign in sides:
        direct[sign].wait_recv()
        gradient = gradient + image_near[s].astype(F32)
    for s, sign in sides:
        hop[sign, True].wait_recv()
        hop[sign, False].wait_recv()
        gradient = gradient + image_hop[s].astype(F32)
    grad_image_ref[...] = project(image_unit, image_inv, gradient)

    gradient = of_line(0)
    for a in (2, 1, 3):
        last[a].wait_recv()
        gradient = gradient + text_near[a].astype(F32)
    grad_text_ref[...] = project(text_unit, text_inv, gradient)

    others(loss_b, 7).wait()
    total = jnp.sum(sums[0:1, :], axis=1, keepdims=True) + jnp.sum(loss_b[...], axis=0)[0:1, 0:1]
    loss_ref[...] = jnp.broadcast_to(total * (LN2 / (2.0 * ROWS * BLOCK)), (1, LANES))
    for cp in started + pending:
        cp.wait_send()
    for sem, ref in enumerate((row_stats, col_stats, loss_a, loss_b)):
        others(ref, 2 * sem).wait()


def text_rows_of(ref, index):
    return ref.at[pl.ds(pl.multiple_of(index * SHARD, SHARD), SHARD), :]


def body(image_embed, text_embed, logit_scale):
    loss, grad_image, grad_text = pl.pallas_call(
        kernel,
        name="contrastive",
        out_shape=(
            jax.ShapeDtypeStruct((1, LANES), F32),
            jax.ShapeDtypeStruct((SHARD, WIDTH), F32),
            jax.ShapeDtypeStruct((SHARD, WIDTH), F32),
        ),
        in_specs=[
            pl.BlockSpec(memory_space=pl.ANY),
            pl.BlockSpec(memory_space=pl.ANY),
            pl.BlockSpec(memory_space=pltpu.SMEM),
        ],
        out_specs=(pl.BlockSpec(memory_space=pltpu.VMEM),) * 3,
        scratch_shapes=[
            pltpu.VMEM((SHARD, WIDTH), F32),
            pltpu.VMEM((SHARD, WIDTH), F32),
            pltpu.VMEM((SHARD, LANES), F32),
            pltpu.VMEM((SHARD, LANES), F32),
            pltpu.VMEM((BLOCK, WIDTH), BF16),
            pltpu.VMEM((BLOCK, WIDTH), BF16),
            pltpu.VMEM((BLOCK, BLOCK), F32),
            pltpu.VMEM((ZS, BLOCK), F32),
            pltpu.VMEM((BLOCK, BLOCK), BF16),
            pltpu.VMEM((16, 8, LANES), F32),
            pltpu.VMEM((16, 8, LANES), F32),
            pltpu.VMEM((8, LANES), F32),
            pltpu.VMEM((16, 8, LANES), F32),
            pltpu.VMEM((16, 8, LANES), F32),
            pltpu.VMEM((ZS, 2, SHARD, WIDTH), BF16),
            pltpu.VMEM((ZS, SHARD, WIDTH), BF16),
            pltpu.VMEM((ZS, SHARD, WIDTH), BF16),
            pltpu.VMEM((2, SHARD, WIDTH), BF16),
            pltpu.VMEM((2, SHARD, WIDTH), BF16),
            pltpu.VMEM((2, SHARD, HALF), BF16),
            pltpu.VMEM((2, SHARD, WIDTH), BF16),
            pltpu.VMEM((BLOCK, WIDTH), BF16),
            pltpu.VMEM((3, 4, SHARD, WIDTH), BF16),
            pltpu.VMEM((4, SHARD, WIDTH), BF16),
            pltpu.VMEM((4, SHARD, WIDTH), BF16),
            pltpu.SemaphoreType.DMA((2,)),
            pltpu.SemaphoreType.DMA((42,)),
            pltpu.SemaphoreType.DMA((42,)),
            pltpu.SemaphoreType.DMA((8,)),
            pltpu.SemaphoreType.DMA((32,)),
            pltpu.SemaphoreType.DMA((32,)),
        ],
        compiler_params=pltpu.CompilerParams(
            collective_id=0, has_side_effects=True, vmem_limit_bytes=60 << 20
        ),
    )(image_embed, text_embed, logit_scale)
    return loss[0, 0], grad_image, grad_text


def solution(mesh):
    placed = (P(("row", "col"), None), P(("col", "row"), None), P())
    return jax.shard_map(
        body,
        mesh=mesh,
        in_specs=placed,
        out_specs=(P(), P(("row", "col"), None), P(("col", "row"), None)),
        check_vma=False,
    )
```

```python
import jax
import jax.numpy as jnp
from jax import lax
from jax.experimental import pallas as pl
from jax.experimental.pallas import tpu as pltpu
from jax.sharding import PartitionSpec as P

EPS = 1e-06
LOG2E = 1.4426950408889634
LN2 = 0.6931471805599453
MESH = pl.DeviceIdType.MESH
F32 = jnp.float32
BF16 = jnp.bfloat16
SHARD, WIDTH, BLOCK, LANES = 48, 768, 768, 128
PAIR = 2 * SHARD
HALF = WIDTH // 2
ROWS, COLS, ZS = 16, 16, 8
ORDER = (4, 3, -3, 2, -2, 1, -1, 0)
SLOT = {d: s for s, d in enumerate(ORDER)} | {-4: 0}


def kernel(
    image_hbm, text_hbm, scale_ref, loss_ref, grad_image_ref, grad_text_ref,
    image_unit, text_unit, image_inv, text_inv, image_all, text_all, logits, col_parts, dlogits,
    row_stats, col_stats, row_merged, loss_a, loss_b,
    image_part, image_other, image_sum, image_hop, image_far, image_half, image_near,
    text_part, text_line, text_hop, text_near,
    in_sem, gather_send, gather_recv, stat_sem, reduce_send, reduce_recv,
):
    r = lax.axis_index("row")
    c = lax.axis_index("col")
    x, y = r // 4, r % 4
    z, k = c // 2, c % 2
    a_pos, b_pos = x + k * (y - x), y + k * (x - y)
    a_step, b_step = 4 - 3 * k, 1 + 3 * k

    def line(a, b):
        return a * a_step + b * b_step

    def on_a(a):
        return (line((a_pos + a) % 4, b_pos), c)

    def on_b(b):
        return (line(a_pos, (b_pos + b) % 4), c)

    def up(d):
        return (r, ((z + d + ZS) % ZS) * 2 + k)

    sibling = (r, z * 2 + 1 - k)

    def copy(src, dst, send, recv, device):
        return pltpu.make_async_remote_copy(
            src_ref=src, dst_ref=dst, send_sem=send, recv_sem=recv,
            device_id=device, device_id_type=MESH,
        )

    loads = [
        pltpu.make_async_copy(image_hbm, image_unit, in_sem.at[0]),
        pltpu.make_async_copy(text_hbm, text_unit, in_sem.at[1]),
    ]
    for load in loads:
        load.start()
    barrier = pltpu.get_barrier_semaphore()
    partners = [up(d) for d in (2, -2, 1, -1)] + [sibling]
    partners += [on_a(a) for a in (1, 2, 3)] + [on_b(b) for b in (1, 2, 3)]
    for device in partners:
        pl.semaphore_signal(barrier, inc=1, device_id=device, device_id_type=MESH)

    def text_rows(index):
        return text_all.at[pl.ds(pl.multiple_of(index * SHARD, SHARD), SHARD), :]

    def image_rows(d):
        first = SLOT[d] * PAIR + k * SHARD
        return image_all.at[pl.ds(pl.multiple_of(first, SHARD), SHARD), :]

    def normalise(ref, inv_ref):
        rows = ref[...]
        inverse = lax.rsqrt(jnp.sum(rows * rows, axis=1, keepdims=True) + EPS)
        unit = rows * inverse
        ref[...] = unit
        inv_ref[...] = jnp.broadcast_to(inverse, (SHARD, LANES))
        return unit.astype(BF16)

    row_stats[0] = jnp.zeros((8, LANES), F32)
    col_stats[0] = jnp.zeros((8, LANES), F32)
    loads[0].wait()
    image_rows(0)[...] = normalise(image_unit, image_inv)
    pl.semaphore_wait(barrier, len(partners))

    started = []

    def gather(src, dst, index, device):
        cp = copy(src, dst, gather_send.at[index], gather_recv.at[index], device)
        cp.start()
        started.append(cp)
        return cp

    def half_of(block, which):
        return block.at[:, which * HALF:(which + 1) * HALF]

    def share(d, index):
        return gather(image_rows(d), image_rows(d), index, sibling)

    sides = ((0, 1), (1, -1))
    ahead = {}
    hops = {}
    near = {}
    across = []
    ends = []
    for turn in range(2):
        for s, sign in sides:
            h = (s + turn) % 2
            ahead[turn, sign] = gather(
                half_of(image_rows(0), h), half_of(image_rows(-2 * sign), h), 4 * s + turn, up(2 * sign)
            )
    loads[1].wait()
    text_own = text_rows(r)
    text_own[...] = normalise(text_unit, text_inv)
    for a in (1, 3, 2):
        near[a] = gather(text_own, text_own, 16 + a, on_a(a))
    for s, sign in sides:
        hops[sign] = gather(image_rows(0), image_rows(-sign), 4 * s + 2, up(sign))

    def pass_text(a):
        block = text_rows(line((a_pos + 4 - a) % 4, b_pos))
        for b in (2, 1, 3):
            across.append(gather(block, block, 20 + 4 * a + b, on_b(b)))

    pass_text(0)
    shares = [share(0, 8)]

    def pass_image(turn):
        for s, sign in sides:
            h = (s + turn) % 2
            ahead[turn, sign].wait_recv()
            block = half_of(image_rows(-2 * sign), h)
            if turn == 0:
                ends.append(gather(block, half_of(image_rows(4), h), 36 + s, up(2 * sign)))
            ends.append(gather(block, half_of(image_rows(-3 * sign), h), 38 + 2 * s + turn, up(sign)))

    for a in (1, 3):
        near[a].wait_recv()
        pass_text(a)
    pass_image(0)
    near[2].wait_recv()
    pass_text(2)
    for s, sign in sides:
        hops[sign].wait_recv()
        shares.append(share(-sign, 9 + s))
    pass_image(1)
    for s, sign in sides:
        shares.append(share(-2 * sign, 11 + s))
    for cp in ends:
        cp.wait_recv()
    for d, index in ((3, 13), (-3, 14), (4, 15)):
        shares.append(share(d, index))
    for cp in across + shares:
        cp.wait_recv()

    scale = scale_ref[0]
    scale2 = scale * LOG2E
    apart = lax.broadcasted_iota(jnp.int32, (PAIR, BLOCK), 1) - lax.broadcasted_iota(
        jnp.int32, (PAIR, BLOCK), 0
    )
    lane = lax.broadcasted_iota(jnp.int32, (PAIR, LANES), 1)
    off_diagonal = (r != c).astype(jnp.int32) * (2 * BLOCK)

    def z_of(d):
        return (z + d + ZS) % ZS

    def own_pairs(s):
        return apart == z_of(ORDER[s]) * PAIR + off_diagonal

    row_lse = jnp.zeros((PAIR, LANES), F32)
    diagonal = jnp.zeros((1, BLOCK), F32)
    for h in range(2):
        rows = slice(h * HALF, (h + 1) * HALF)
        logits[rows, :] = scale2 * lax.dot_general(
            image_all[rows, :], text_all[...], (((1,), (1,)), ((), ())),
            preferred_element_type=F32,
        )
        for s in range(4 * h, 4 * h + 4):
            block = logits[s * PAIR:(s + 1) * PAIR, :]
            row_max = jnp.max(block, axis=1, keepdims=True)
            row_sum = jnp.sum(jnp.exp2(block - row_max), axis=1, keepdims=True)
            row_lse = jnp.where(lane == s, row_max + jnp.log2(row_sum), row_lse)
            col_max = jnp.max(block, axis=0, keepdims=True)
            col_sum = jnp.sum(jnp.exp2(block - col_max), axis=0, keepdims=True)
            col_parts[s:s + 1, :] = col_max + jnp.log2(col_sum)
    row_lse = row_lse.T
    for s in range(ZS):
        row_stats[0, pl.ds(z_of(ORDER[s]), 1), 0:PAIR] = row_lse[s:s + 1, :]
    parts = col_parts[...]
    top = jnp.max(parts, axis=0, keepdims=True)
    merged = top + jnp.log2(jnp.sum(jnp.exp2(parts - top), axis=0, keepdims=True))
    for q in range(6):
        col_stats[0, q:q + 1, :] = merged[:, q * LANES:(q + 1) * LANES]

    col_offsets = [(d, other) for d in ORDER for other in (0, 1) if (d, other) != (0, 0)]
    row_offsets = [(a, b) for a in (2, 1, 3, 0) for b in (2, 1, 3, 0) if (a, b) != (0, 0)]
    row_offsets.sort(key=lambda ab: -min(ab[0], 4 - ab[0]) - min(ab[1], 4 - ab[1]))

    def col_peer(i):
        d, other = col_offsets[i]
        return (r, z_of(d) * 2 + (k + other) % 2)

    def row_peer(i):
        a, b = row_offsets[i]
        return (line((a_pos + a) % 4, (b_pos + b) % 4), c)

    def send_to(ref, sem, peer, i):
        copy(
            ref.at[0], ref.at[i + 1], stat_sem.at[2 * sem], stat_sem.at[2 * sem + 1], peer(i)
        ).start()

    def spread(ref, sem, peer):
        for i in range(15):
            send_to(ref, sem, peer, i)

    def others(ref, sem):
        return pltpu.make_async_copy(ref.at[1:16], ref.at[1:16], stat_sem.at[sem])

    def combine(every):
        most = jnp.max(every, axis=0)
        return most + jnp.log2(jnp.sum(jnp.exp2(every - most[None]), axis=0))

    for i in range(15):
        send_to(row_stats, 0, col_peer, i)
        send_to(col_stats, 1, row_peer, i)
    for s in range(ZS):
        block = logits[s * PAIR:(s + 1) * PAIR, :]
        diagonal = diagonal + jnp.sum(jnp.where(own_pairs(s), block, 0.0), axis=0, keepdims=True)
    others(row_stats, 1).wait()
    others(col_stats, 3).wait()

    row_merged[...] = combine(row_stats[...])
    col_lse = combine(col_stats[...])
    ordered = jnp.concatenate([row_merged[pl.ds(z_of(d), 1), :] for d in ORDER], axis=0)
    lse_columns = ordered.T
    col_row = jnp.concatenate([col_lse[q:q + 1, :] for q in range(6)], axis=1)

    pending = []

    def reduce(src, dst, index, device):
        cp = copy(src, dst, reduce_send.at[index], reduce_recv.at[index], device)
        cp.start()
        pending.append(cp)
        return cp

    def gradient_of(t):
        for s in (2 * t, 2 * t + 1):
            rows = slice(s * PAIR, (s + 1) * PAIR)
            block = logits[rows, :]
            total = jnp.exp2(block - lse_columns[0:PAIR, s:s + 1]) + jnp.exp2(block - col_row)
            total = total - jnp.where(own_pairs(s), 2.0, 0.0)
            dlogits[rows, :] = (0.5 * total).astype(BF16)

    swaps = {}

    def image_terms(t):
        part = scale * jnp.dot(
            dlogits[2 * t * PAIR:(2 * t + 2) * PAIR, :], text_all[...], preferred_element_type=F32
        )
        image_part[2 * t:2 * t + 2] = part.astype(BF16).reshape(2, 2, SHARD, WIDTH)
        swaps[t] = reduce(
            image_part.at[2 * t:2 * t + 2, 1 - k], image_other.at[2 * t:2 * t + 2], 12 + t, sibling
        )

    def text_terms(h):
        rows = slice(h * HALF, (h + 1) * HALF)
        part = scale * lax.dot_general(
            dlogits[:, rows], image_all[...], (((0,), (0,)), ((), ())), preferred_element_type=F32
        )
        text_part[rows, :] = part.astype(BF16)

    def of_z(d):
        s = SLOT[d]
        return image_part[s, k].astype(F32) + image_other[s].astype(F32)

    def summed(d):
        image_sum[SLOT[d]] = of_z(d).astype(BF16)
        return image_sum.at[SLOT[d]]

    quarter = {}
    far = {}
    direct = {}
    gradient_of(0)
    image_terms(0)
    gradient_of(1)
    image_terms(1)
    gradient_of(2)
    gradient_of(3)
    text_terms(0)
    swaps[0].wait_recv()
    swaps[1].wait_recv()
    for s, sign in sides:
        far[sign] = reduce(summed(3 * sign), image_far.at[s], 3 + s, up(sign))
    block = summed(4)
    for s, sign in sides:
        quarter[sign] = reduce(half_of(block, s), image_half.at[s], 1 + s, up(2 * sign))
    text_terms(1)
    lines = {}
    for a in (2, 1, 3, 0):
        for b in (2, 1, 3):
            lines[a, b] = reduce(
                text_rows_of(text_part, line((a_pos + a) % 4, (b_pos + b) % 4)),
                text_line.at[b - 1, a], 16 + 4 * b + a, on_b(b),
            )
    col_total = jnp.sum(col_lse[0:6, :], axis=0, keepdims=True)
    on_block = jnp.sum(diagonal, axis=1, keepdims=True)
    loss_a[0] = jnp.concatenate(
        [col_total, jnp.broadcast_to(on_block, (1, LANES)), jnp.zeros((6, LANES), F32)], axis=0
    )
    spread(loss_a, 2, col_peer)

    image_terms(2)
    image_terms(3)
    swaps[2].wait_recv()
    direct[1] = reduce(summed(1), image_near.at[0], 5, up(1))
    swaps[3].wait_recv()
    direct[-1] = reduce(summed(-1), image_near.at[1], 6, up(-1))

    def of_line(a):
        for b in (1, 2, 3):
            lines[a, b].wait_recv()
        total = text_rows_of(text_part, line((a_pos + a) % 4, b_pos))[...].astype(F32)
        for b in range(3):
            total = total + text_line[b, a].astype(F32)
        return total

    last = {}

    def pass_line(a):
        text_hop[a] = of_line(a).astype(BF16)
        last[a] = reduce(text_hop.at[a], text_near.at[a], 8 + a, on_a(a))

    hop = {}

    def pass_sum(sign, s, half, early):
        cols = slice(half * HALF, (half + 1) * HALF)
        at = SLOT[2 * sign]
        both = image_part[at, k, :, cols].astype(F32) + image_other[at, :, cols].astype(F32)
        both = both + image_far[s, :, cols].astype(F32)
        if not early:
            both = both + image_half[s].astype(F32)
        image_sum[at, :, cols] = both.astype(BF16)
        hop[sign, early] = reduce(
            image_sum.at[at, :, cols], image_hop.at[s, :, cols], 7 + s if early else 17 + s, up(2 * sign)
        )

    for s, sign in sides:
        far[sign].wait_recv()
        pass_sum(sign, s, 1 - s, True)
    pass_line(2)
    for s, sign in sides:
        quarter[sign].wait_recv()
        pass_sum(sign, s, s, False)
    others(loss_a, 5).wait()
    sums = jnp.sum(loss_a[...], axis=0)
    row_total = jnp.sum(row_merged[:, 0:PAIR], axis=0, keepdims=True)
    row_total = jnp.sum(row_total, axis=1, keepdims=True) - 2.0 * sums[1:2, 0:1]
    loss_b[0] = jnp.broadcast_to(row_total, (8, LANES))
    spread(loss_b, 3, row_peer)

    pass_line(1)

    pass_line(3)

    def project(unit_ref, inv_ref, gradient):
        unit = unit_ref[...]
        along = jnp.sum(unit * gradient, axis=1, keepdims=True)
        return inv_ref[:, 0:1] * (gradient - unit * along)

    gradient = of_z(0)
    for s, sign in sides:
        direct[sign].wait_recv()
        gradient = gradient + image_near[s].astype(F32)
    for s, sign in sides:
        hop[sign, True].wait_recv()
        hop[sign, False].wait_recv()
        gradient = gradient + image_hop[s].astype(F32)
    grad_image_ref[...] = project(image_unit, image_inv, gradient)

    gradient = of_line(0)
    for a in (2, 1, 3):
        last[a].wait_recv()
        gradient = gradient + text_near[a].astype(F32)
    grad_text_ref[...] = project(text_unit, text_inv, gradient)

    others(loss_b, 7).wait()
    total = jnp.sum(sums[0:1, :], axis=1, keepdims=True) + jnp.sum(loss_b[...], axis=0)[0:1, 0:1]
    loss_ref[...] = jnp.broadcast_to(total * (LN2 / (2.0 * ROWS * BLOCK)), (1, LANES))
    for cp in started + pending:
        cp.wait_send()
    for sem, ref in enumerate((row_stats, col_stats, loss_a, loss_b)):
        others(ref, 2 * sem).wait()


def text_rows_of(ref, index):
    return ref.at[pl.ds(pl.multiple_of(index * SHARD, SHARD), SHARD), :]


def body(image_embed, text_embed, logit_scale):
    loss, grad_image, grad_text = pl.pallas_call(
        kernel,
        name="contrastive",
        out_shape=(
            jax.ShapeDtypeStruct((1, LANES), F32),
            jax.ShapeDtypeStruct((SHARD, WIDTH), F32),
            jax.ShapeDtypeStruct((SHARD, WIDTH), F32),
        ),
        in_specs=[
            pl.BlockSpec(memory_space=pl.ANY),
            pl.BlockSpec(memory_space=pl.ANY),
            pl.BlockSpec(memory_space=pltpu.SMEM),
        ],
        out_specs=(pl.BlockSpec(memory_space=pltpu.VMEM),) * 3,
        scratch_shapes=[
            pltpu.VMEM((SHARD, WIDTH), F32),
            pltpu.VMEM((SHARD, WIDTH), F32),
            pltpu.VMEM((SHARD, LANES), F32),
            pltpu.VMEM((SHARD, LANES), F32),
            pltpu.VMEM((BLOCK, WIDTH), BF16),
            pltpu.VMEM((BLOCK, WIDTH), BF16),
            pltpu.VMEM((BLOCK, BLOCK), F32),
            pltpu.VMEM((ZS, BLOCK), F32),
            pltpu.VMEM((BLOCK, BLOCK), BF16),
            pltpu.VMEM((16, 8, LANES), F32),
            pltpu.VMEM((16, 8, LANES), F32),
            pltpu.VMEM((8, LANES), F32),
            pltpu.VMEM((16, 8, LANES), F32),
            pltpu.VMEM((16, 8, LANES), F32),
            pltpu.VMEM((ZS, 2, SHARD, WIDTH), BF16),
            pltpu.VMEM((ZS, SHARD, WIDTH), BF16),
            pltpu.VMEM((ZS, SHARD, WIDTH), BF16),
            pltpu.VMEM((2, SHARD, WIDTH), BF16),
            pltpu.VMEM((2, SHARD, WIDTH), BF16),
            pltpu.VMEM((2, SHARD, HALF), BF16),
            pltpu.VMEM((2, SHARD, WIDTH), BF16),
            pltpu.VMEM((BLOCK, WIDTH), BF16),
            pltpu.VMEM((3, 4, SHARD, WIDTH), BF16),
            pltpu.VMEM((4, SHARD, WIDTH), BF16),
            pltpu.VMEM((4, SHARD, WIDTH), BF16),
            pltpu.SemaphoreType.DMA((2,)),
            pltpu.SemaphoreType.DMA((42,)),
            pltpu.SemaphoreType.DMA((42,)),
            pltpu.SemaphoreType.DMA((8,)),
            pltpu.SemaphoreType.DMA((32,)),
            pltpu.SemaphoreType.DMA((32,)),
        ],
        compiler_params=pltpu.CompilerParams(
            collective_id=0, has_side_effects=True, vmem_limit_bytes=32 << 20
        ),
    )(
        pltpu.with_memory_space_constraint(image_embed, pltpu.HBM),
        pltpu.with_memory_space_constraint(text_embed, pltpu.HBM),
        logit_scale,
    )
    return loss[0, 0], grad_image, grad_text


def solution(mesh):
    placed = (P(("row", "col"), None), P(("col", "row"), None), P())
    return jax.shard_map(
        body,
        mesh=mesh,
        in_specs=placed,
        out_specs=(P(), P(("row", "col"), None), P(("col", "row"), None)),
        check_vma=False,
    )
```

```python
import jax
import jax.numpy as jnp
from jax import lax
from jax.experimental import pallas as pl
from jax.experimental.pallas import tpu as pltpu
from jax.sharding import PartitionSpec as P

EPS = 1e-06
LOG2E = 1.4426950408889634
LN2 = 0.6931471805599453
MESH = pl.DeviceIdType.MESH
F32 = jnp.float32
BF16 = jnp.bfloat16
SHARD, WIDTH, BLOCK, LANES = 48, 768, 768, 128
PAIR = 2 * SHARD
HALF = WIDTH // 2
ROWS, COLS, ZS = 16, 16, 8
ORDER = (4, 3, -3, 2, -2, 1, -1, 0)
SLOT = {d: s for s, d in enumerate(ORDER)} | {-4: 0}


def kernel(
    image_hbm, text_hbm, scale_ref, loss_ref, grad_image_ref, grad_text_ref,
    image_unit, text_unit, image_inv, text_inv, image_all, text_all, logits, col_parts, dlogits,
    row_stats, col_stats, row_merged, loss_pair, loss_a, loss_b,
    image_part, image_other, image_sum, image_hop, image_far, image_half, image_near,
    text_part, text_line, text_hop, text_near,
    in_sem, gather_send, gather_recv, stat_sem, pair_sem, reduce_send, reduce_recv,
):
    r = lax.axis_index("row")
    c = lax.axis_index("col")
    x, y = r // 4, r % 4
    z, k = c // 2, c % 2
    a_pos, b_pos = x + k * (y - x), y + k * (x - y)
    a_step, b_step = 4 - 3 * k, 1 + 3 * k

    def line(a, b):
        return a * a_step + b * b_step

    def on_a(a):
        return (line((a_pos + a) % 4, b_pos), c)

    def on_b(b):
        return (line(a_pos, (b_pos + b) % 4), c)

    def up(d):
        return (r, ((z + d + ZS) % ZS) * 2 + k)

    sibling = (r, z * 2 + 1 - k)

    def copy(src, dst, send, recv, device):
        return pltpu.make_async_remote_copy(
            src_ref=src, dst_ref=dst, send_sem=send, recv_sem=recv,
            device_id=device, device_id_type=MESH,
        )

    loads = [
        pltpu.make_async_copy(image_hbm, image_unit, in_sem.at[0]),
        pltpu.make_async_copy(text_hbm, text_unit, in_sem.at[1]),
    ]
    for load in loads:
        load.start()
    barrier = pltpu.get_barrier_semaphore()
    partners = [up(d) for d in (2, -2, 1, -1)] + [sibling]
    partners += [on_a(a) for a in (1, 2, 3)] + [on_b(b) for b in (1, 2, 3)]
    for device in partners:
        pl.semaphore_signal(barrier, inc=1, device_id=device, device_id_type=MESH)

    def text_rows(index):
        return text_all.at[pl.ds(pl.multiple_of(index * SHARD, SHARD), SHARD), :]

    def image_rows(d):
        first = SLOT[d] * PAIR + k * SHARD
        return image_all.at[pl.ds(pl.multiple_of(first, SHARD), SHARD), :]

    def normalise(ref, inv_ref):
        rows = ref[...]
        inverse = lax.rsqrt(jnp.sum(rows * rows, axis=1, keepdims=True) + EPS)
        unit = rows * inverse
        ref[...] = unit
        inv_ref[...] = jnp.broadcast_to(inverse, (SHARD, LANES))
        return unit.astype(BF16)

    row_stats[0] = jnp.zeros((8, LANES), F32)
    col_stats[0] = jnp.zeros((8, LANES), F32)
    loads[0].wait()
    image_rows(0)[...] = normalise(image_unit, image_inv)
    pl.semaphore_wait(barrier, len(partners))

    started = []

    def gather(src, dst, index, device):
        cp = copy(src, dst, gather_send.at[index], gather_recv.at[index], device)
        cp.start()
        started.append(cp)
        return cp

    def half_of(block, which):
        return block.at[:, which * HALF:(which + 1) * HALF]

    def share(d, index):
        return gather(image_rows(d), image_rows(d), index, sibling)

    sides = ((0, 1), (1, -1))
    ahead = {}
    hops = {}
    near = {}
    across = []
    ends = []
    loads[1].wait()
    text_own = text_rows(r)
    text_own[...] = normalise(text_unit, text_inv)
    for a in (1, 3, 2):
        near[a] = gather(text_own, text_own, 16 + a, on_a(a))
    for turn in range(2):
        for s, sign in sides:
            h = (s + turn) % 2
            ahead[turn, sign] = gather(
                half_of(image_rows(0), h), half_of(image_rows(-2 * sign), h), 4 * s + turn, up(2 * sign)
            )
    for s, sign in sides:
        hops[sign] = gather(image_rows(0), image_rows(-sign), 4 * s + 2, up(sign))

    def pass_text(a):
        block = text_rows(line((a_pos + 4 - a) % 4, b_pos))
        for b in (2, 1, 3):
            across.append(gather(block, block, 20 + 4 * a + b, on_b(b)))

    pass_text(0)
    shares = [share(0, 8)]

    def pass_image(turn):
        for s, sign in sides:
            h = (s + turn) % 2
            ahead[turn, sign].wait_recv()
            block = half_of(image_rows(-2 * sign), h)
            if turn == 0:
                ends.append(gather(block, half_of(image_rows(4), h), 36 + s, up(2 * sign)))
            ends.append(gather(block, half_of(image_rows(-3 * sign), h), 38 + 2 * s + turn, up(sign)))

    for a in (1, 3):
        near[a].wait_recv()
        pass_text(a)
    pass_image(0)
    near[2].wait_recv()
    pass_text(2)
    for s, sign in sides:
        hops[sign].wait_recv()
        shares.append(share(-sign, 9 + s))
    pass_image(1)
    for s, sign in sides:
        shares.append(share(-2 * sign, 11 + s))
    for cp in ends:
        cp.wait_recv()
    for d, index in ((3, 13), (-3, 14), (4, 15)):
        shares.append(share(d, index))
    for cp in across + shares:
        cp.wait_recv()

    scale = scale_ref[0]
    scale2 = scale * LOG2E
    apart = lax.broadcasted_iota(jnp.int32, (PAIR, BLOCK), 1) - lax.broadcasted_iota(
        jnp.int32, (PAIR, BLOCK), 0
    )
    lane = lax.broadcasted_iota(jnp.int32, (PAIR, LANES), 1)
    off_diagonal = (r != c).astype(jnp.int32) * (2 * BLOCK)

    def z_of(d):
        return (z + d + ZS) % ZS

    def own_pairs(s):
        return apart == z_of(ORDER[s]) * PAIR + off_diagonal

    row_lse = jnp.zeros((PAIR, LANES), F32)
    diagonal = jnp.zeros((1, BLOCK), F32)
    for h in range(2):
        rows = slice(h * HALF, (h + 1) * HALF)
        logits[rows, :] = scale2 * lax.dot_general(
            image_all[rows, :], text_all[...], (((1,), (1,)), ((), ())),
            preferred_element_type=F32,
        )
        for s in range(4 * h, 4 * h + 4):
            block = logits[s * PAIR:(s + 1) * PAIR, :]
            row_max = jnp.max(block, axis=1, keepdims=True)
            row_sum = jnp.sum(jnp.exp2(block - row_max), axis=1, keepdims=True)
            row_lse = jnp.where(lane == s, row_max + jnp.log2(row_sum), row_lse)
            col_max = jnp.max(block, axis=0, keepdims=True)
            col_sum = jnp.sum(jnp.exp2(block - col_max), axis=0, keepdims=True)
            col_parts[s:s + 1, :] = col_max + jnp.log2(col_sum)
    row_lse = row_lse.T
    for s in range(ZS):
        row_stats[0, pl.ds(z_of(ORDER[s]), 1), 0:PAIR] = row_lse[s:s + 1, :]
    parts = col_parts[...]
    top = jnp.max(parts, axis=0, keepdims=True)
    merged = top + jnp.log2(jnp.sum(jnp.exp2(parts - top), axis=0, keepdims=True))
    for q in range(6):
        col_stats[0, q:q + 1, :] = merged[:, q * LANES:(q + 1) * LANES]

    col_offsets = [(d, other) for d in ORDER for other in (0, 1) if (d, other) != (0, 0)]
    row_offsets = [(a, b) for a in (2, 1, 3, 0) for b in (2, 1, 3, 0) if (a, b) != (0, 0)]
    row_offsets.sort(key=lambda ab: -min(ab[0], 4 - ab[0]) - min(ab[1], 4 - ab[1]))

    def col_peer(i):
        d, other = col_offsets[i]
        return (r, z_of(d) * 2 + (k + other) % 2)

    def row_peer(i):
        a, b = row_offsets[i]
        return (line((a_pos + a) % 4, (b_pos + b) % 4), c)

    def send_to(ref, sem, peer, i):
        copy(
            ref.at[0], ref.at[i + 1], stat_sem.at[2 * sem], stat_sem.at[2 * sem + 1], peer(i)
        ).start()

    def spread(ref, sem, peer):
        for i in range(15):
            send_to(ref, sem, peer, i)

    def others(ref, sem):
        return pltpu.make_async_copy(ref.at[1:16], ref.at[1:16], stat_sem.at[sem])

    def combine(every):
        most = jnp.max(every, axis=0)
        return most + jnp.log2(jnp.sum(jnp.exp2(every - most[None]), axis=0))

    for i in range(15):
        send_to(row_stats, 0, col_peer, i)
        send_to(col_stats, 1, row_peer, i)
    for s in range(ZS):
        block = logits[s * PAIR:(s + 1) * PAIR, :]
        diagonal = diagonal + jnp.sum(jnp.where(own_pairs(s), block, 0.0), axis=0, keepdims=True)
    for cp in started:
        cp.wait_send()
    others(row_stats, 1).wait()
    others(col_stats, 3).wait()

    row_merged[...] = combine(row_stats[...])
    col_lse = combine(col_stats[...])
    ordered = jnp.concatenate([row_merged[pl.ds(z_of(d), 1), :] for d in ORDER], axis=0)
    lse_columns = ordered.T
    col_row = jnp.concatenate([col_lse[q:q + 1, :] for q in range(6)], axis=1)

    col_total = jnp.sum(col_lse[0:6, :], axis=0, keepdims=True)
    on_block = jnp.sum(diagonal, axis=1, keepdims=True)
    loss_pair[0] = jnp.concatenate(
        [col_total, jnp.broadcast_to(on_block, (1, LANES)), jnp.zeros((6, LANES), F32)], axis=0
    )
    pair = copy(loss_pair.at[0], loss_pair.at[1], pair_sem.at[0], pair_sem.at[1], sibling)
    pair.start()

    pending = []

    def reduce(src, dst, index, device):
        cp = copy(src, dst, reduce_send.at[index], reduce_recv.at[index], device)
        cp.start()
        pending.append(cp)
        return cp

    def gradient_of(t):
        for s in (2 * t, 2 * t + 1):
            rows = slice(s * PAIR, (s + 1) * PAIR)
            block = logits[rows, :]
            total = jnp.exp2(block - lse_columns[0:PAIR, s:s + 1]) + jnp.exp2(block - col_row)
            total = total - jnp.where(own_pairs(s), 2.0, 0.0)
            dlogits[rows, :] = (0.5 * total).astype(BF16)

    swaps = {}

    def image_terms(t):
        part = scale * jnp.dot(
            dlogits[2 * t * PAIR:(2 * t + 2) * PAIR, :], text_all[...], preferred_element_type=F32
        )
        image_part[2 * t:2 * t + 2] = part.astype(BF16).reshape(2, 2, SHARD, WIDTH)
        swaps[t] = reduce(
            image_part.at[2 * t:2 * t + 2, 1 - k], image_other.at[2 * t:2 * t + 2], 12 + t, sibling
        )

    def text_terms(h):
        rows = slice(h * HALF, (h + 1) * HALF)
        part = scale * lax.dot_general(
            dlogits[:, rows], image_all[...], (((0,), (0,)), ((), ())), preferred_element_type=F32
        )
        text_part[rows, :] = part.astype(BF16)

    def of_z(d):
        s = SLOT[d]
        return image_part[s, k].astype(F32) + image_other[s].astype(F32)

    def summed(d):
        image_sum[SLOT[d]] = of_z(d).astype(BF16)
        return image_sum.at[SLOT[d]]

    quarter = {}
    far = {}
    direct = {}
    gradient_of(0)
    image_terms(0)
    gradient_of(1)
    image_terms(1)
    gradient_of(2)
    gradient_of(3)
    text_terms(0)
    text_terms(1)
    lines = {}
    for a in (2, 1, 3, 0):
        for b in (2, 1, 3):
            lines[a, b] = reduce(
                text_rows_of(text_part, line((a_pos + a) % 4, (b_pos + b) % 4)),
                text_line.at[b - 1, a], 16 + 4 * b + a, on_b(b),
            )
    pair.wait_recv()
    loss_a[0] = jnp.sum(loss_pair[...], axis=0)
    for i in range(1, ZS):
        copy(loss_a.at[0], loss_a.at[i], stat_sem.at[4], stat_sem.at[5], up(i)).start()

    def loss_z(sem):
        return pltpu.make_async_copy(loss_a.at[1:ZS], loss_a.at[1:ZS], stat_sem.at[sem])

    swaps[0].wait_recv()
    swaps[1].wait_recv()
    for s, sign in sides:
        far[sign] = reduce(summed(3 * sign), image_far.at[s], 3 + s, up(sign))
    block = summed(4)
    for s, sign in sides:
        quarter[sign] = reduce(half_of(block, s), image_half.at[s], 1 + s, up(2 * sign))
    image_terms(2)
    image_terms(3)
    swaps[2].wait_recv()
    direct[1] = reduce(summed(1), image_near.at[0], 5, up(1))
    swaps[3].wait_recv()
    direct[-1] = reduce(summed(-1), image_near.at[1], 6, up(-1))

    def of_line(a):
        for b in (1, 2, 3):
            lines[a, b].wait_recv()
        total = text_rows_of(text_part, line((a_pos + a) % 4, b_pos))[...].astype(F32)
        for b in range(3):
            total = total + text_line[b, a].astype(F32)
        return total

    last = {}

    def pass_line(a):
        text_hop[a] = of_line(a).astype(BF16)
        last[a] = reduce(text_hop.at[a], text_near.at[a], 8 + a, on_a(a))

    hop = {}

    def pass_sum(sign, s, half, early):
        cols = slice(half * HALF, (half + 1) * HALF)
        at = SLOT[2 * sign]
        both = image_part[at, k, :, cols].astype(F32) + image_other[at, :, cols].astype(F32)
        both = both + image_far[s, :, cols].astype(F32)
        if not early:
            both = both + image_half[s].astype(F32)
        image_sum[at, :, cols] = both.astype(BF16)
        hop[sign, early] = reduce(
            image_sum.at[at, :, cols], image_hop.at[s, :, cols], 7 + s if early else 17 + s, up(2 * sign)
        )

    loss_z(5).wait()
    sums = jnp.sum(loss_a[...], axis=0)
    row_total = jnp.sum(row_merged[:, 0:PAIR], axis=0, keepdims=True)
    row_total = jnp.sum(row_total, axis=1, keepdims=True) - 2.0 * sums[1:2, 0:1]
    loss_b[0] = jnp.broadcast_to(row_total, (8, LANES))
    spread(loss_b, 3, row_peer)

    for s, sign in sides:
        far[sign].wait_recv()
        pass_sum(sign, s, 1 - s, True)
    pass_line(2)
    for s, sign in sides:
        quarter[sign].wait_recv()
        pass_sum(sign, s, s, False)
    pass_line(1)

    pass_line(3)

    late = list(last.values()) + list(hop.values())
    for cp in pending:
        if all(cp is not other for other in late):
            cp.wait_send()
    for sem, ref in ((0, row_stats), (1, col_stats)):
        others(ref, 2 * sem).wait()
    pair.wait_send()
    loss_z(4).wait()

    def project(unit_ref, inv_ref, gradient):
        unit = unit_ref[...]
        along = jnp.sum(unit * gradient, axis=1, keepdims=True)
        return inv_ref[:, 0:1] * (gradient - unit * along)

    gradient = of_z(0)
    for s, sign in sides:
        direct[sign].wait_recv()
        gradient = gradient + image_near[s].astype(F32)
    for s, sign in sides:
        hop[sign, True].wait_recv()
        hop[sign, False].wait_recv()
        gradient = gradient + image_hop[s].astype(F32)
    grad_image_ref[...] = project(image_unit, image_inv, gradient)

    gradient = of_line(0)
    for a in (2, 1, 3):
        last[a].wait_recv()
        gradient = gradient + text_near[a].astype(F32)
    grad_text_ref[...] = project(text_unit, text_inv, gradient)

    others(loss_b, 7).wait()
    total = jnp.sum(sums[0:1, :], axis=1, keepdims=True) + jnp.sum(loss_b[...], axis=0)[0:1, 0:1]
    loss_ref[...] = jnp.broadcast_to(total * (LN2 / (2.0 * ROWS * BLOCK)), (1, LANES))
    others(loss_b, 6).wait()
    for cp in list(last.values()) + list(hop.values()):
        cp.wait_send()


def text_rows_of(ref, index):
    return ref.at[pl.ds(pl.multiple_of(index * SHARD, SHARD), SHARD), :]


def body(image_embed, text_embed, logit_scale):
    loss, grad_image, grad_text = pl.pallas_call(
        kernel,
        name="contrastive",
        out_shape=(
            jax.ShapeDtypeStruct((1, LANES), F32),
            jax.ShapeDtypeStruct((SHARD, WIDTH), F32),
            jax.ShapeDtypeStruct((SHARD, WIDTH), F32),
        ),
        in_specs=[
            pl.BlockSpec(memory_space=pl.ANY),
            pl.BlockSpec(memory_space=pl.ANY),
            pl.BlockSpec(memory_space=pltpu.SMEM),
        ],
        out_specs=(pl.BlockSpec(memory_space=pltpu.VMEM),) * 3,
        scratch_shapes=[
            pltpu.VMEM((SHARD, WIDTH), F32),
            pltpu.VMEM((SHARD, WIDTH), F32),
            pltpu.VMEM((SHARD, LANES), F32),
            pltpu.VMEM((SHARD, LANES), F32),
            pltpu.VMEM((BLOCK, WIDTH), BF16),
            pltpu.VMEM((BLOCK, WIDTH), BF16),
            pltpu.VMEM((BLOCK, BLOCK), F32),
            pltpu.VMEM((ZS, BLOCK), F32),
            pltpu.VMEM((BLOCK, BLOCK), BF16),
            pltpu.VMEM((16, 8, LANES), F32),
            pltpu.VMEM((16, 8, LANES), F32),
            pltpu.VMEM((8, LANES), F32),
            pltpu.VMEM((2, 8, LANES), F32),
            pltpu.VMEM((ZS, 8, LANES), F32),
            pltpu.VMEM((16, 8, LANES), F32),
            pltpu.VMEM((ZS, 2, SHARD, WIDTH), BF16),
            pltpu.VMEM((ZS, SHARD, WIDTH), BF16),
            pltpu.VMEM((ZS, SHARD, WIDTH), BF16),
            pltpu.VMEM((2, SHARD, WIDTH), BF16),
            pltpu.VMEM((2, SHARD, WIDTH), BF16),
            pltpu.VMEM((2, SHARD, HALF), BF16),
            pltpu.VMEM((2, SHARD, WIDTH), BF16),
            pltpu.VMEM((BLOCK, WIDTH), BF16),
            pltpu.VMEM((3, 4, SHARD, WIDTH), BF16),
            pltpu.VMEM((4, SHARD, WIDTH), BF16),
            pltpu.VMEM((4, SHARD, WIDTH), BF16),
            pltpu.SemaphoreType.DMA((2,)),
            pltpu.SemaphoreType.DMA((42,)),
            pltpu.SemaphoreType.DMA((42,)),
            pltpu.SemaphoreType.DMA((8,)),
            pltpu.SemaphoreType.DMA((2,)),
            pltpu.SemaphoreType.DMA((32,)),
            pltpu.SemaphoreType.DMA((32,)),
        ],
        compiler_params=pltpu.CompilerParams(
            collective_id=0, has_side_effects=True, vmem_limit_bytes=32 << 20
        ),
    )(
        pltpu.with_memory_space_constraint(image_embed, pltpu.HBM),
        pltpu.with_memory_space_constraint(text_embed, pltpu.HBM),
        logit_scale,
    )
    return loss[0, 0], grad_image, grad_text


def solution(mesh):
    placed = (P(("row", "col"), None), P(("col", "row"), None), P())
    return jax.shard_map(
        body,
        mesh=mesh,
        in_specs=placed,
        out_specs=(P(), P(("row", "col"), None), P(("col", "row"), None)),
        check_vma=False,
    )
```

```python
import jax
import jax.numpy as jnp
from jax import lax
from jax.experimental import pallas as pl
from jax.experimental.pallas import tpu as pltpu
from jax.sharding import PartitionSpec as P

EPS = 1e-06
LOG2E = 1.4426950408889634
LN2 = 0.6931471805599453
MESH = pl.DeviceIdType.MESH
F32 = jnp.float32
BF16 = jnp.bfloat16
SHARD, WIDTH, BLOCK, LANES = 48, 768, 768, 128
PAIR = 2 * SHARD
HALF = WIDTH // 2
ROWS, COLS, ZS = 16, 16, 8
ORDER = (4, 3, -3, 2, -2, 1, -1, 0)
SLOT = {d: s for s, d in enumerate(ORDER)} | {-4: 0}


def kernel(
    image_hbm, text_hbm, scale_ref, loss_ref, grad_image_ref, grad_text_ref,
    image_unit, text_unit, image_inv, text_inv, image_all, text_all, logits, col_parts, dlogits,
    row_stats, col_stats, row_merged, loss_pair, loss_a, loss_b,
    image_part, image_other, image_sum, image_hop, image_far, image_half, image_near,
    text_part, text_line, text_hop, text_near,
    in_sem, gather_send, gather_recv, stat_sem, pair_sem, reduce_send, reduce_recv,
):
    r = lax.axis_index("row")
    c = lax.axis_index("col")
    x, y = r // 4, r % 4
    z, k = c // 2, c % 2
    a_pos, b_pos = x + k * (y - x), y + k * (x - y)
    a_step, b_step = 4 - 3 * k, 1 + 3 * k

    def line(a, b):
        return a * a_step + b * b_step

    def on_a(a):
        return (line((a_pos + a) % 4, b_pos), c)

    def on_b(b):
        return (line(a_pos, (b_pos + b) % 4), c)

    def up(d):
        return (r, ((z + d + ZS) % ZS) * 2 + k)

    sibling = (r, z * 2 + 1 - k)

    def copy(src, dst, send, recv, device):
        return pltpu.make_async_remote_copy(
            src_ref=src, dst_ref=dst, send_sem=send, recv_sem=recv,
            device_id=device, device_id_type=MESH,
        )

    loads = [
        pltpu.make_async_copy(image_hbm, image_unit, in_sem.at[0]),
        pltpu.make_async_copy(text_hbm, text_unit, in_sem.at[1]),
    ]
    for load in loads:
        load.start()
    barrier = pltpu.get_barrier_semaphore()
    partners = [up(d) for d in (2, -2, 1, -1)] + [sibling]
    partners += [on_a(a) for a in (1, 2, 3)] + [on_b(b) for b in (1, 2, 3)]
    for device in partners:
        pl.semaphore_signal(barrier, inc=1, device_id=device, device_id_type=MESH)

    def text_rows(index):
        return text_all.at[pl.ds(pl.multiple_of(index * SHARD, SHARD), SHARD), :]

    def image_rows(d):
        first = SLOT[d] * PAIR + k * SHARD
        return image_all.at[pl.ds(pl.multiple_of(first, SHARD), SHARD), :]

    def normalise(ref, inv_ref):
        rows = ref[...]
        inverse = lax.rsqrt(jnp.sum(rows * rows, axis=1, keepdims=True) + EPS)
        unit = rows * inverse
        ref[...] = unit
        inv_ref[...] = jnp.broadcast_to(inverse, (SHARD, LANES))
        return unit.astype(BF16)

    row_stats[0] = jnp.zeros((8, LANES), F32)
    loads[0].wait()
    image_rows(0)[...] = normalise(image_unit, image_inv)
    pl.semaphore_wait(barrier, len(partners))

    started = []

    def gather(src, dst, index, device):
        cp = copy(src, dst, gather_send.at[index], gather_recv.at[index], device)
        cp.start()
        started.append(cp)
        return cp

    def half_of(block, which):
        return block.at[:, which * HALF:(which + 1) * HALF]

    def share(d, index):
        return gather(image_rows(d), image_rows(d), index, sibling)

    sides = ((0, 1), (1, -1))
    ahead = {}
    hops = {}
    near = {}
    across = []
    ends = []
    loads[1].wait()
    text_own = text_rows(r)
    text_own[...] = normalise(text_unit, text_inv)
    for a in (1, 3, 2):
        near[a] = gather(text_own, text_own, 16 + a, on_a(a))
    for turn in range(2):
        for s, sign in sides:
            h = (s + turn) % 2
            ahead[turn, sign] = gather(
                half_of(image_rows(0), h), half_of(image_rows(-2 * sign), h), 4 * s + turn, up(2 * sign)
            )
    for s, sign in sides:
        hops[sign] = gather(image_rows(0), image_rows(-sign), 4 * s + 2, up(sign))

    def pass_text(a):
        block = text_rows(line((a_pos + 4 - a) % 4, b_pos))
        for b in (2, 1, 3):
            across.append(gather(block, block, 20 + 4 * a + b, on_b(b)))

    pass_text(0)
    shares = [share(0, 8)]

    def pass_image(turn):
        for s, sign in sides:
            h = (s + turn) % 2
            ahead[turn, sign].wait_recv()
            block = half_of(image_rows(-2 * sign), h)
            if turn == 0:
                ends.append(gather(block, half_of(image_rows(4), h), 36 + s, up(2 * sign)))
            ends.append(gather(block, half_of(image_rows(-3 * sign), h), 38 + 2 * s + turn, up(sign)))

    for a in (1, 3):
        near[a].wait_recv()
        pass_text(a)
    pass_image(0)
    near[2].wait_recv()
    pass_text(2)
    pass_image(1)
    for s, sign in sides:
        hops[sign].wait_recv()
        shares.append(share(-sign, 9 + s))
    for s, sign in sides:
        shares.append(share(-2 * sign, 11 + s))
    for cp in ends:
        cp.wait_recv()
    for d, index in ((3, 13), (-3, 14), (4, 15)):
        shares.append(share(d, index))
    for cp in across + shares:
        cp.wait_recv()

    scale = scale_ref[0]
    scale2 = scale * LOG2E
    apart = lax.broadcasted_iota(jnp.int32, (PAIR, BLOCK), 1) - lax.broadcasted_iota(
        jnp.int32, (PAIR, BLOCK), 0
    )
    lane = lax.broadcasted_iota(jnp.int32, (PAIR, LANES), 1)
    off_diagonal = (r != c).astype(jnp.int32) * (2 * BLOCK)

    def z_of(d):
        return (z + d + ZS) % ZS

    def own_pairs(s):
        return apart == z_of(ORDER[s]) * PAIR + off_diagonal

    row_lse = jnp.zeros((PAIR, LANES), F32)
    diagonal = jnp.zeros((1, BLOCK), F32)
    for h in range(2):
        rows = slice(h * HALF, (h + 1) * HALF)
        logits[rows, :] = scale2 * lax.dot_general(
            image_all[rows, :], text_all[...], (((1,), (1,)), ((), ())),
            preferred_element_type=F32,
        )
        for s in range(4 * h, 4 * h + 4):
            block = logits[s * PAIR:(s + 1) * PAIR, :]
            row_max = jnp.max(block, axis=1, keepdims=True)
            row_sum = jnp.sum(jnp.exp2(block - row_max), axis=1, keepdims=True)
            row_lse = jnp.where(lane == s, row_max + jnp.log2(row_sum), row_lse)
            col_max = jnp.max(block, axis=0, keepdims=True)
            col_sum = jnp.sum(jnp.exp2(block - col_max), axis=0, keepdims=True)
            col_parts[s:s + 1, :] = col_max + jnp.log2(col_sum)
    row_lse = row_lse.T
    for s in range(ZS):
        row_stats[0, pl.ds(z_of(ORDER[s]), 1), 0:PAIR] = row_lse[s:s + 1, :]
    parts = col_parts[...]
    top = jnp.max(parts, axis=0, keepdims=True)
    merged = top + jnp.log2(jnp.sum(jnp.exp2(parts - top), axis=0, keepdims=True))
    for q in range(6):
        col_stats[0, q:q + 1, :] = merged[:, q * LANES:(q + 1) * LANES]

    col_offsets = [(d, other) for d in ORDER for other in (0, 1) if (d, other) != (0, 0)]
    row_offsets = [(a, b) for a in (2, 1, 3, 0) for b in (2, 1, 3, 0) if (a, b) != (0, 0)]
    row_offsets.sort(key=lambda ab: -min(ab[0], 4 - ab[0]) - min(ab[1], 4 - ab[1]))

    def col_peer(i):
        d, other = col_offsets[i]
        return (r, z_of(d) * 2 + (k + other) % 2)

    def row_peer(i):
        a, b = row_offsets[i]
        return (line((a_pos + a) % 4, (b_pos + b) % 4), c)

    def send_to(ref, sem, peer, i):
        copy(
            ref.at[0], ref.at[i + 1], stat_sem.at[2 * sem], stat_sem.at[2 * sem + 1], peer(i)
        ).start()

    def spread(ref, sem, peer):
        for i in range(15):
            send_to(ref, sem, peer, i)

    def others(ref, sem):
        return pltpu.make_async_copy(ref.at[1:16], ref.at[1:16], stat_sem.at[sem])

    def combine(every):
        most = jnp.max(every, axis=0)
        return most + jnp.log2(jnp.sum(jnp.exp2(every - most[None]), axis=0))

    for i in range(15):
        send_to(row_stats, 0, col_peer, i)
        send_to(col_stats, 1, row_peer, i)
    for s in range(ZS):
        block = logits[s * PAIR:(s + 1) * PAIR, :]
        diagonal = diagonal + jnp.sum(jnp.where(own_pairs(s), block, 0.0), axis=0, keepdims=True)
    for cp in started:
        cp.wait_send()
    others(row_stats, 1).wait()
    others(col_stats, 3).wait()

    row_merged[...] = combine(row_stats[...])
    col_lse = combine(col_stats[...])
    ordered = jnp.concatenate([row_merged[pl.ds(z_of(d), 1), :] for d in ORDER], axis=0)
    lse_columns = ordered.T
    col_row = jnp.concatenate([col_lse[q:q + 1, :] for q in range(6)], axis=1)

    col_total = jnp.sum(col_lse[0:6, :], axis=0, keepdims=True)
    on_block = jnp.sum(diagonal, axis=1, keepdims=True)
    loss_pair[0] = jnp.concatenate(
        [col_total, jnp.broadcast_to(on_block, (1, LANES)), jnp.zeros((6, LANES), F32)], axis=0
    )
    pair = copy(loss_pair.at[0], loss_pair.at[1], pair_sem.at[0], pair_sem.at[1], sibling)
    pair.start()

    pending = []

    def reduce(src, dst, index, device):
        cp = copy(src, dst, reduce_send.at[index], reduce_recv.at[index], device)
        cp.start()
        pending.append(cp)
        return cp

    def gradient_of(t):
        for s in (2 * t, 2 * t + 1):
            rows = slice(s * PAIR, (s + 1) * PAIR)
            block = logits[rows, :]
            total = jnp.exp2(block - lse_columns[0:PAIR, s:s + 1]) + jnp.exp2(block - col_row)
            total = total - jnp.where(own_pairs(s), 2.0, 0.0)
            dlogits[rows, :] = (0.5 * total).astype(BF16)

    swaps = {}

    def image_terms(t):
        part = scale * jnp.dot(
            dlogits[2 * t * PAIR:(2 * t + 2) * PAIR, :], text_all[...], preferred_element_type=F32
        )
        image_part[2 * t:2 * t + 2] = part.astype(BF16).reshape(2, 2, SHARD, WIDTH)
        swaps[t] = reduce(
            image_part.at[2 * t:2 * t + 2, 1 - k], image_other.at[2 * t:2 * t + 2], 12 + t, sibling
        )

    def text_terms(h):
        rows = slice(h * HALF, (h + 1) * HALF)
        part = scale * lax.dot_general(
            dlogits[:, rows], image_all[...], (((0,), (0,)), ((), ())), preferred_element_type=F32
        )
        text_part[rows, :] = part.astype(BF16)

    def of_z(d):
        s = SLOT[d]
        return image_part[s, k].astype(F32) + image_other[s].astype(F32)

    def summed(d):
        image_sum[SLOT[d]] = of_z(d).astype(BF16)
        return image_sum.at[SLOT[d]]

    quarter = {}
    far = {}
    direct = {}
    gradient_of(0)
    image_terms(0)
    gradient_of(1)
    image_terms(1)
    gradient_of(2)
    gradient_of(3)
    text_terms(0)
    text_terms(1)
    lines = {}
    for a in (2, 1, 3, 0):
        for b in (2, 1, 3):
            lines[a, b] = reduce(
                text_rows_of(text_part, line((a_pos + a) % 4, (b_pos + b) % 4)),
                text_line.at[b - 1, a], 16 + 4 * b + a, on_b(b),
            )
    pair.wait_recv()
    loss_a[0] = jnp.sum(loss_pair[...], axis=0)
    for i in range(1, ZS):
        copy(loss_a.at[0], loss_a.at[i], stat_sem.at[4], stat_sem.at[5], up(i)).start()

    def loss_z(sem):
        return pltpu.make_async_copy(loss_a.at[1:ZS], loss_a.at[1:ZS], stat_sem.at[sem])

    swaps[0].wait_recv()
    swaps[1].wait_recv()
    for s, sign in sides:
        far[sign] = reduce(summed(3 * sign), image_far.at[s], 3 + s, up(sign))
    block = summed(4)
    for s, sign in sides:
        quarter[sign] = reduce(half_of(block, s), image_half.at[s], 1 + s, up(2 * sign))
    image_terms(2)
    image_terms(3)
    swaps[2].wait_recv()
    direct[1] = reduce(summed(1), image_near.at[0], 5, up(1))
    swaps[3].wait_recv()
    direct[-1] = reduce(summed(-1), image_near.at[1], 6, up(-1))

    def of_line(a):
        for b in (1, 2, 3):
            lines[a, b].wait_recv()
        total = text_rows_of(text_part, line((a_pos + a) % 4, b_pos))[...].astype(F32)
        for b in range(3):
            total = total + text_line[b, a].astype(F32)
        return total

    last = {}

    def pass_line(a):
        text_hop[a] = of_line(a).astype(BF16)
        last[a] = reduce(text_hop.at[a], text_near.at[a], 8 + a, on_a(a))

    hop = {}

    def pass_sum(sign, s, half, early):
        cols = slice(half * HALF, (half + 1) * HALF)
        at = SLOT[2 * sign]
        both = image_part[at, k, :, cols].astype(F32) + image_other[at, :, cols].astype(F32)
        both = both + image_far[s, :, cols].astype(F32)
        if not early:
            both = both + image_half[s].astype(F32)
        image_sum[at, :, cols] = both.astype(BF16)
        hop[sign, early] = reduce(
            image_sum.at[at, :, cols], image_hop.at[s, :, cols], 7 + s if early else 17 + s, up(2 * sign)
        )

    for s, sign in sides:
        far[sign].wait_recv()
        pass_sum(sign, s, 1 - s, True)
    pass_line(2)
    loss_z(5).wait()
    sums = jnp.sum(loss_a[...], axis=0)
    row_total = jnp.sum(row_merged[:, 0:PAIR], axis=0, keepdims=True)
    row_total = jnp.sum(row_total, axis=1, keepdims=True) - 2.0 * sums[1:2, 0:1]
    loss_b[0] = jnp.broadcast_to(row_total, (8, LANES))
    spread(loss_b, 3, row_peer)

    for s, sign in sides:
        quarter[sign].wait_recv()
        pass_sum(sign, s, s, False)
    pass_line(1)

    pass_line(3)

    late = list(last.values()) + list(hop.values())
    for cp in pending:
        if all(cp is not other for other in late):
            cp.wait_send()
    for sem, ref in ((0, row_stats), (1, col_stats)):
        others(ref, 2 * sem).wait()
    pair.wait_send()
    loss_z(4).wait()

    def project(unit_ref, inv_ref, gradient):
        unit = unit_ref[...]
        along = jnp.sum(unit * gradient, axis=1, keepdims=True)
        return inv_ref[:, 0:1] * (gradient - unit * along)

    gradient = of_z(0)
    for s, sign in sides:
        direct[sign].wait_recv()
        gradient = gradient + image_near[s].astype(F32)
    for s, sign in sides:
        hop[sign, True].wait_recv()
        hop[sign, False].wait_recv()
        gradient = gradient + image_hop[s].astype(F32)
    grad_image_ref[...] = project(image_unit, image_inv, gradient)

    gradient = of_line(0)
    for a in (2, 1, 3):
        last[a].wait_recv()
        gradient = gradient + text_near[a].astype(F32)
    grad_text_ref[...] = project(text_unit, text_inv, gradient)

    others(loss_b, 7).wait()
    total = jnp.sum(sums[0:1, :], axis=1, keepdims=True) + jnp.sum(loss_b[...], axis=0)[0:1, 0:1]
    loss_ref[...] = jnp.broadcast_to(total * (LN2 / (2.0 * ROWS * BLOCK)), (1, LANES))
    others(loss_b, 6).wait()
    for cp in list(last.values()) + list(hop.values()):
        cp.wait_send()


def text_rows_of(ref, index):
    return ref.at[pl.ds(pl.multiple_of(index * SHARD, SHARD), SHARD), :]


def body(image_embed, text_embed, logit_scale):
    loss, grad_image, grad_text = pl.pallas_call(
        kernel,
        name="contrastive",
        out_shape=(
            jax.ShapeDtypeStruct((1, LANES), F32),
            jax.ShapeDtypeStruct((SHARD, WIDTH), F32),
            jax.ShapeDtypeStruct((SHARD, WIDTH), F32),
        ),
        in_specs=[
            pl.BlockSpec(memory_space=pl.ANY),
            pl.BlockSpec(memory_space=pl.ANY),
            pl.BlockSpec(memory_space=pltpu.SMEM),
        ],
        out_specs=(pl.BlockSpec(memory_space=pltpu.VMEM),) * 3,
        scratch_shapes=[
            pltpu.VMEM((SHARD, WIDTH), F32),
            pltpu.VMEM((SHARD, WIDTH), F32),
            pltpu.VMEM((SHARD, LANES), F32),
            pltpu.VMEM((SHARD, LANES), F32),
            pltpu.VMEM((BLOCK, WIDTH), BF16),
            pltpu.VMEM((BLOCK, WIDTH), BF16),
            pltpu.VMEM((BLOCK, BLOCK), F32),
            pltpu.VMEM((ZS, BLOCK), F32),
            pltpu.VMEM((BLOCK, BLOCK), BF16),
            pltpu.VMEM((16, 8, LANES), F32),
            pltpu.VMEM((16, 6, LANES), F32),
            pltpu.VMEM((8, LANES), F32),
            pltpu.VMEM((2, 8, LANES), F32),
            pltpu.VMEM((ZS, 8, LANES), F32),
            pltpu.VMEM((16, 8, LANES), F32),
            pltpu.VMEM((ZS, 2, SHARD, WIDTH), BF16),
            pltpu.VMEM((ZS, SHARD, WIDTH), BF16),
            pltpu.VMEM((ZS, SHARD, WIDTH), BF16),
            pltpu.VMEM((2, SHARD, WIDTH), BF16),
            pltpu.VMEM((2, SHARD, WIDTH), BF16),
            pltpu.VMEM((2, SHARD, HALF), BF16),
            pltpu.VMEM((2, SHARD, WIDTH), BF16),
            pltpu.VMEM((BLOCK, WIDTH), BF16),
            pltpu.VMEM((3, 4, SHARD, WIDTH), BF16),
            pltpu.VMEM((4, SHARD, WIDTH), BF16),
            pltpu.VMEM((4, SHARD, WIDTH), BF16),
            pltpu.SemaphoreType.DMA((2,)),
            pltpu.SemaphoreType.DMA((42,)),
            pltpu.SemaphoreType.DMA((42,)),
            pltpu.SemaphoreType.DMA((8,)),
            pltpu.SemaphoreType.DMA((2,)),
            pltpu.SemaphoreType.DMA((32,)),
            pltpu.SemaphoreType.DMA((32,)),
        ],
        compiler_params=pltpu.CompilerParams(
            collective_id=0, has_side_effects=True, vmem_limit_bytes=32 << 20
        ),
    )(
        pltpu.with_memory_space_constraint(image_embed, pltpu.HBM),
        pltpu.with_memory_space_constraint(text_embed, pltpu.HBM),
        logit_scale,
    )
    return loss[0, 0], grad_image, grad_text


def solution(mesh):
    placed = (P(("row", "col"), None), P(("col", "row"), None), P())
    return jax.shard_map(
        body,
        mesh=mesh,
        in_specs=placed,
        out_specs=(P(), P(("row", "col"), None), P(("col", "row"), None)),
        check_vma=False,
    )
```
